256 devices in a mesh: scen: 4 (over x_lo, core), row: 8 (over x_hi, y), col: 8 (over z).
Axes of the slice: x: 4 (x_hi: 2, x_lo: 2; x = x_hi * 2 + x_lo), y: 4, z: 8, core: 2. Of those that a mesh axis runs over, the one named last changes fastest.
Arguments:
- link_block: float32 [2560, 2, 8, 8, 128], P('scen', None, 'row', 'col'), may hold values from -0.15625 to 0.15625
- block_mask: int32 [32, 2, 8, 8], P('scen', None, 'row', 'col'), may hold values 0 or 1
- barrier_diag: float32 [2560], P('scen'), may hold values from 0.1 to 10
- first_section_diag: float32 [2, 8, 8, 128], P(None, 'row', 'col'), may hold values from 0.5 to 1.5
Outputs:
- factored: float32 [2, 8, 8, 128, 2, 8, 8, 128], P(None, 'row', 'scen', None, None, None, 'col')
The draws below stay inside these ranges and needn't reach their ends.
All inputs are finite; a program needn't handle non-finite values. No bound on the sum of `block_mask` on one device may be relied on, other than what follows from the above.
Results may differ from the reference program's by a relative error of at most 0.0003.
Values sent between devices are 32-bit elements; how exact they have to be, the bound alone decides.
A program may use at most 128 MiB of HBM per device.

```python
import math
import jax
import jax.numpy as jnp
from jax import lax

ORDER = 16384
TB = 128
PANEL = 256
ROWS_SC = 80
SCENS = 32
ROWS = 2560
AB = 2
N_ROW = 8
N_COL = 8


def with_ends(values, key, low, largest):
    longest = values.shape.index(max(values.shape))
    spots = []
    for shift in (0, 1):
        where = [jax.random.randint(jax.random.fold_in(key, axis), (), 0, length) for axis, length in enumerate(values.shape)]
        where[longest] = (where[longest] + shift) % values.shape[longest]
        spots.append(tuple(where))
    return values.at[spots[0]].set(low).at[spots[1]].set(largest)


def with_spikes(array, rng, source, target, blocks, factor):
    def block_of(axis_at):
        return (jnp.arange(array.shape[axis_at]) // (array.shape[axis_at] // blocks)).reshape((-1,) + (1,) * (array.ndim - 1 - axis_at))

    near = jax.random.permutation(rng, blocks)[block_of(target)]
    far = (block_of(target) + blocks // 2) % blocks
    return jnp.where((block_of(source) == near) | (block_of(source) == far), factor * array, array)


def level_of(own_key, dims, shards, least, high):
    def one(position, blocks):
        steps = jax.random.uniform(jax.random.fold_in(jax.random.fold_in(own_key, 6), position), (blocks,), jnp.float32, least / len(shards), high / len(shards))
        return jnp.repeat(jnp.exp(steps), dims[position] // blocks).reshape((-1,) + (1,) * (len(dims) - position - 1))

    level = one(*shards[0])
    for cut in shards[1:]:
        level = level * one(*cut)
    return level


def gaussian_with(rng, dims, deviation, limit, pieces, heavy, kind=jnp.bfloat16):
    entries = deviation * jax.random.normal(rng, dims, jnp.float32)
    if pieces:
        entries = entries * level_of(rng, dims, pieces, -0.22, 0.18)
    return jnp.clip(with_spikes(entries, jax.random.fold_in(rng, 3), *heavy), -limit, limit).astype(kind)


def setup_inputs(seed: int = 0) -> dict:
    key_of = jax.random.split(jax.random.key(seed), 5)
    return {
        "link_block": gaussian_with(key_of[0], (ROWS, AB, N_ROW, N_COL, TB), ROWS ** -0.5, 0.15625, ((0, 4), (2, 8), (3, 8)), (0, 3, 8, 2.0), jnp.float32),
        "block_mask": with_ends((jax.random.randint(key_of[1], (SCENS, AB, N_ROW, N_COL), 0, 3) < 2).astype(jnp.int32), jax.random.fold_in(key_of[1], 1), 0, 1),
        "barrier_diag": jnp.clip(jnp.exp(math.log(10.0) - 4.6051702 * jax.random.uniform(key_of[2], (ROWS,), jnp.float32) ** level_of(key_of[2], (ROWS,), ((0, 4),), -0.2, 0.2)), 0.1, 10.0),
        "first_section_diag": jnp.clip(0.5 + 1.0 * jax.random.uniform(key_of[3], (AB, N_ROW, N_COL, TB), jnp.float32) ** level_of(key_of[3], (AB, N_ROW, N_COL, TB), ((1, 8), (2, 8)), -0.2, 0.2), 0.5, 1.5),
    }


HIGH = lax.Precision.HIGHEST

def solve_right(lower, rhs):
    return jax.scipy.linalg.solve_triangular(lower, rhs.T, lower=True).T

def reference(link_block, block_mask, barrier_diag, first_section_diag):
    total_rows = link_block.shape[0]
    mask_rows = jnp.repeat(block_mask.astype(jnp.float32), ROWS_SC, axis=0)
    masked = (link_block * mask_rows[..., None]).reshape(total_rows, ORDER)
    scaled = masked * barrier_diag[:, None]
    schur = lax.dot_general(masked.astype(jnp.float32), scaled.astype(jnp.float32), (((0,), (0,)), ((), ())), precision=HIGH, preferred_element_type=jnp.float32)
    places = jnp.arange(ORDER)
    schur = schur.at[places, places].add(first_section_diag.reshape(ORDER))
    width = 2 * PANEL
    row_ids = jnp.arange(ORDER)[:, None]
    panel_ids = jnp.arange(PANEL)[None, :]
    first_factor = jnp.linalg.cholesky(schur[:PANEL, :PANEL])
    first = jnp.where(row_ids >= panel_ids, solve_right(first_factor, schur[:, :PANEL]), 0.0)
    coupling = first[PANEL:width]
    second_in = schur[:, PANEL:width] - jnp.dot(first.astype(jnp.float32), coupling.T.astype(jnp.float32), precision=HIGH, preferred_element_type=jnp.float32)
    second_factor = jnp.linalg.cholesky(second_in[PANEL:width])
    second = jnp.where(row_ids >= panel_ids + PANEL, solve_right(second_factor, second_in), 0.0)
    factor = jnp.concatenate([first, second], axis=1)
    update = schur[:, width:] - jnp.dot(factor.astype(jnp.float32), factor[width:].T.astype(jnp.float32), precision=HIGH, preferred_element_type=jnp.float32)
    trailing = jnp.where(row_ids >= width, update, schur[:, width:])
    result = jnp.concatenate([factor, trailing], axis=1)
    return result.reshape(AB, N_ROW, N_COL, TB, AB, N_ROW, N_COL, TB)
```

```python
import functools
import jax
import jax.numpy as jnp
from jax import lax
from jax.experimental import pallas as pl
from jax.experimental.pallas import tpu as pltpu
from jax.sharding import PartitionSpec as P

PANEL = 256
F32 = jnp.float32
BF16 = jnp.bfloat16
KL = 640
KP = 648
HALVES = ((0, 320), (320, 328))


def place():
    s = lax.axis_index("scen")
    r = lax.axis_index("row")
    z = lax.axis_index("col")
    return (r // 4) * 2 + s // 2, r % 4, z, s % 2


def device(x, y, z, p):
    return ((x % 2) * 2 + p, (x // 2) * 4 + y, z)


def remote(src, dst, send, recv, to):
    return pltpu.make_async_remote_copy(
        src_ref=src, dst_ref=dst, send_sem=send, recv_sem=recv,
        device_id=to, device_id_type=pl.DeviceIdType.MESH,
    )


def split(v):
    hi = v.astype(BF16)
    return hi, (v - hi.astype(F32)).astype(BF16)


def mm(a, b):
    return jnp.dot(a, b, preferred_element_type=F32)


def nt(a, b):
    return lax.dot_general(a, b, (((1,), (1,)), ((), ())), preferred_element_type=F32)


def dot32(a, b):
    return jnp.dot(a, b, precision=lax.Precision.HIGHEST, preferred_element_type=F32)


def factor_tile(t):
    lanes = lax.broadcasted_iota(jnp.int32, (8, 128), 1)
    for p in range(0, 128, 8):
        n = 128 - p
        cols = [jnp.broadcast_to(t[p:128, p + j:p + j + 1], (n, 128)) for j in range(8)]
        row = t[p:p + 8, :]
        subl = lax.broadcasted_iota(jnp.int32, (8, 128), 0)
        us, rs_ = [], []
        for j in range(8):
            inv = lax.rsqrt(cols[j][j:j + 1, :])
            u = cols[j] * inv
            r = jnp.where(lanes[0:1] == p + j, inv, row[j:j + 1, :] * inv)
            scal = [u[m:m + 1, :] for m in range(8)]
            for m in range(j + 1, 8):
                cols[m] = cols[m] - u * scal[m]
            uj = jnp.where(subl > j, u[0:8, :], 0.0)
            base = jnp.where(jnp.logical_and(lanes == p + j, subl > j), 0.0, row)
            row = jnp.where(subl == j, jnp.broadcast_to(r, (8, 128)), base - uj * r)
            us.append(u)
        t[p:p + 8, :] = row
        if n > 8:
            rest = t[p + 8:128, :]
            rl_ = lax.broadcasted_iota(jnp.int32, (n - 8, 128), 1)
            rest = jnp.where(jnp.logical_and(rl_ >= p, rl_ < p + 8), 0.0, rest)
            for j in range(8):
                r = jnp.where(jnp.logical_and(lanes[0:1] > p + j, lanes[0:1] < p + 8), 0.0, row[j:j + 1, :])
                rest = rest - us[j][8:, :] * r
            t[p + 8:128, :] = rest


def factor_lead(m, t):
    ii = lax.broadcasted_iota(jnp.int32, (128, 128), 0)
    jj = lax.broadcasted_iota(jnp.int32, (128, 128), 1)
    for k in range(4):
        a, e = k * 128, (k + 1) * 128
        t[...] = m[a:e, a:e]
        factor_tile(t)
        inv = jnp.where(ii >= jj, t[...], 0.0)
        m[a:e, a:e] = inv
        for j in range(4):
            if j != k:
                m[a:e, j * 128:(j + 1) * 128] = dot32(inv, m[a:e, j * 128:(j + 1) * 128])
        for i in range(k + 1, 4):
            ut = m[a:e, i * 128:(i + 1) * 128].T
            for j in range(4):
                c = slice(j * 128, (j + 1) * 128)
                v = dot32(ut, m[a:e, c])
                r = slice(i * 128, (i + 1) * 128)
                if j == k:
                    m[r, c] = -v
                elif j < k or j >= i or True:
                    m[r, c] = m[r, c] - v


def schur_kernel(
    b, out, rbuf, lbuf, lthi, ltlo, rh, rl, pbuf, qbuf, s_out,
    gsend, grecv, tile, wbuf, li, ms, mf, lih, lil, mfh, mfl,
    s1, sp, s2, s3, sz, sf, sx, rsem, rsem2, lsem, xsem,
    gsem, wsend, wrecv, lsend, lrecv, wsib, lsib, msend, mrecv,
):
    x, y, z, p = place()
    xn = lambda d: device((x + d) % 4, y, z, p)
    yn = lambda d: device(x, (y + d) % 4, z, p)
    zup = device(x, y, (z + 1) % 8, p)
    zdn = device(x, y, (z + 7) % 8, p)
    peer_x = x + 1 - 2 * (x % 2)
    peer = device(peer_x, y, z, p)
    sib = device(x, y, z, 1 - p)
    x_lo = x % 2
    rel = (z + 8 - 4 * x_lo) % 8
    is_src = rel < 4

    is_root = jnp.logical_and(x == 0, y == 0)
    others = jnp.logical_not(is_root)

    barrier = pltpu.get_barrier_semaphore()
    partners = [device((x + i) % 4, (y + j) % 4, z, p) for i in range(4) for j in range(4) if i or j]
    partners += [zup, zdn, sib]
    for to in partners:
        pl.semaphore_signal(barrier, inc=1, device_id=to, device_id_type=pl.DeviceIdType.MESH)
    pl.semaphore_wait(barrier, len(partners))

    full = pl.ds(0, KL)
    sends = []

    def go(copy, cond=None):
        if cond is None:
            copy.start()
        else:
            pl.when(cond)(copy.start)
        sends.append((copy, cond))

    def wait_on(ref, sem):
        pltpu.make_async_copy(ref, ref, sem).wait()

    for a in range(2):
        for h, (lo, n) in enumerate(HALVES):
            rows = pl.ds(lo, n)
            go(remote(b.at[a, rows], lbuf.at[a, x_lo, z % 4, rows], sp.at[a, h],
                      lsem.at[a, x_lo, z % 4, h], peer), jnp.logical_not(is_src))
    for d in (1, 3, 2):
        go(remote(b.at[0, full], rbuf.at[0, x, y], s1.at[0, d - 1], rsem.at[0, x, y], xn(d)))
        go(remote(b.at[1, full], rbuf.at[1, x, y], s1.at[1, d - 1], rsem.at[1, x, y], yn(d)))

    def own(a):
        rbuf[a, x, y] = b[a, 0:KL, :]

    own(0)
    own(1)

    @pl.when(is_src)
    def _():
        for a in range(2):
            lbuf[a, x_lo, z % 4] = b[a]

    up_of = lambda i: jnp.where(i < 2, 2, 5)

    def zsend(q, xl, cond):
        a = q
        for h, (lo, n) in enumerate(HALVES):
            rows = pl.ds(lo, n)
            for dr, to in ((0, zup), (1, zdn)):
                ref = lbuf.at[a, xl, z % 4, rows]
                k = jnp.where(xl == x_lo, 0, 1)
                go(remote(ref, ref, sz.at[a, k, h, dr], lsem.at[a, xl, z % 4, h], to), cond)

    def stage2_send(a, k, d):
        ref = rbuf.at[0, (x + d) % 4, y] if a == 0 else rbuf.at[1, x, (y + d) % 4]
        sem = rsem.at[0, (x + d) % 4, y] if a == 0 else rsem.at[1, x, (y + d) % 4]
        if d:
            wait_on(ref, sem)
        step = yn if a == 0 else xn
        go(remote(ref, ref, s2.at[a, k, 0], sem, step(1)))
        go(remote(ref, ref, s2.at[a, k, 1], sem, step(3)))

    def stage2_forward(a, k, d):
        for dr, e in ((0, 3), (1, 1)):
            i = ((x + d) % 4, (y + e) % 4) if a == 0 else ((x + e) % 4, (y + d) % 4)
            ref = rbuf.at[a, i[0], i[1]]
            wait_on(ref, rsem.at[a, i[0], i[1]])
            rows = pl.ds(dr * 320, 320)
            ref = rbuf.at[a, i[0], i[1], rows]
            sem = (rsem2.at[a, i[0], i[1], dr])
            step = yn if a == 0 else xn
            go(remote(ref, ref, s3.at[a, k, dr], sem, step(1 if dr == 0 else 3)))

    def stage2_last(a, d):
        for dr in range(2):
            i = ((x + d) % 4, (y + 2) % 4) if a == 0 else ((x + 2) % 4, (y + d) % 4)
            wait_on(rbuf.at[a, i[0], i[1], pl.ds(dr * 320, 320)], rsem2.at[a, i[0], i[1], dr])

    def zforward(d):
        for a in range(2):
            for xl in range(2):
                for h, (lo, n) in enumerate(HALVES):
                    rows = pl.ds(lo, n)
                    for dr, to in ((0, zup), (1, zdn)):
                        i = (rel + 8 - d) % 8 if dr == 0 else (rel + d) % 8
                        reach = up_of(i) if dr == 0 else 7 - up_of(i)
                        slot = i % 4
                        valid = jnp.logical_and(i < 4, d <= reach)
                        ref = lbuf.at[a, xl, slot, rows]
                        sem = lsem.at[a, xl, slot, h]

                        @pl.when(valid)
                        def _():
                            wait_on(ref, sem)

                        if d < 5:
                            go(remote(ref, ref, sf.at[d - 1, a, xl, h, dr], sem, to),
                               jnp.logical_and(i < 4, d < reach))

    for a in range(2):
        zsend(a, x_lo, is_src)
    for a in range(2):
        stage2_send(a, 0, 0)
    for a in range(2):
        for h, (lo, n) in enumerate(HALVES):
            @pl.when(is_src)
            def _():
                wait_on(lbuf.at[a, 1 - x_lo, z % 4, pl.ds(lo, n)], lsem.at[a, 1 - x_lo, z % 4, h])
        zsend(a, 1 - x_lo, is_src)
    for k, d in ((1, 1), (2, 3)):
        for a in range(2):
            stage2_send(a, k, d)
    zforward(1)
    for a in range(2):
        stage2_send(a, 3, 2)
        stage2_forward(a, 0, 0)
    zforward(2)
    for k, d in ((1, 1), (2, 3)):
        for a in range(2):
            stage2_forward(a, k, d)
    zforward(3)
    for a in range(2):
        stage2_forward(a, 3, 2)
    zforward(4)
    zforward(5)
    for d in range(4):
        for a in range(2):
            stage2_last(a, d)

    @pl.loop(0, 4)
    def _(hh):
        for a in range(2):
            for xl in range(2):
                hi, lo = split(lbuf[a, xl, hh, 0:KL, :].T)
                rb = pl.multiple_of(((hh // 2) * 4 + a * 2 + hh % 2) * 128, 128)
                lthi[pl.ds(rb, 128), xl * KL:(xl + 1) * KL] = hi
                ltlo[pl.ds(rb, 128), xl * KL:(xl + 1) * KL] = lo

    gcopy = remote(gsend, grecv, gsem.at[0], gsem.at[1], sib)

    @pl.when(is_root)
    def _():
        for j in range(2):
            lead = slice(j * 512, j * 512 + 256)
            cols = slice(j * 256, j * 256 + 256)

            def gram(rows):
                return nt(lthi[rows, :], lthi[lead, :]) + nt(lthi[rows, :], ltlo[lead, :]) + nt(ltlo[rows, :], lthi[lead, :])

            for i in range(2):
                gsend[i * 256:i * 256 + 256, cols] = gram(slice(i * 512, i * 512 + 256))
            there = pl.multiple_of((1 - p) * 512 + 256, 256)
            here = pl.multiple_of(p * 512 + 256, 256)
            gsend[512:768, cols] = gram(pl.ds(there, 256))
            for c in range(2):
                ms[j * 2 + c, 256:512, :] = gram(pl.ds(here, 256))[:, c * 128:(c + 1) * 128]
        gcopy.start()

    def sib_copy(a, g):
        rows = pl.ds(a * 256, 256)
        return remote(pbuf.at[g, rows], qbuf.at[g, rows], sx.at[a, g], xsem.at[a, g], sib)

    def product(a):
        @pl.loop(0, 8)
        def _(g):
            for xl in range(2):
                for c in range(2):
                    hi, lo = split(rbuf[c, (g // 4) * 2 + xl, g % 4])
                    rh[xl * KL:(xl + 1) * KL, c * 128:(c + 1) * 128] = hi
                    rl[xl * KL:(xl + 1) * KL, c * 128:(c + 1) * 128] = lo
            for t in range(2):
                q = (1 - p) if t == 0 else p
                rows = pl.ds(pl.multiple_of(q * 512 + a * 256, 256), 256)
                v = mm(lthi[rows, :], rh[...]) + mm(ltlo[rows, :], rh[...]) + mm(lthi[rows, :], rl[...])
                if t == 0:
                    pbuf[g, a * 256:(a + 1) * 256, :] = v
                    sib_copy(a, g).start()
                else:
                    s_out[g, a * 256:(a + 1) * 256, :] = v

    def combine(a):
        rows = slice(a * 256, a * 256 + 256)

        @pl.loop(0, 8)
        def _(g):
            sib_copy(a, g).wait_recv()
            s_out[g, rows, :] = s_out[g, rows, :] + qbuf[g, rows, :]

        @pl.when(z // 2 == x_lo * 2 + p)
        def _():
            ii = lax.broadcasted_iota(jnp.int32, (128, 128), 0)
            jj = lax.broadcasted_iota(jnp.int32, (128, 128), 1)
            g = (x // 2) * 4 + y
            here = pl.ds(pl.multiple_of(a * 256 + (z % 2) * 128, 128), 128)
            diag = jnp.where(ii == jj, b[a, KL:KL + 1, :], 0.0)
            s_out[g, here, a * 128:(a + 1) * 128] += diag

    def not_root(i, j):
        return jnp.logical_not(jnp.logical_and(i == 0, j == 0))

    def make_spread(piece, send, recv):
        def copy(i, j, to_i, to_j, slot):
            ref = piece(i, j)
            return remote(ref, ref, send.at[slot], recv.at[i, j], device(to_i, to_j, z, p))

        def scatter():
            for k in range(1, 16):
                go(copy(k // 4, k % 4, k // 4, k % 4, k), is_root)

        def arrived(i, j):
            pl.when(others)(lambda: wait_on(piece(i, j), recv.at[i, j]))

        def along_x():
            arrived(x, y)
            for d in (1, 3, 2):
                i = (x + d) % 4
                go(copy(x, y, i, y, 15 + d), not_root(i, y))

        def along_y():
            for e in range(4):
                i = (x + e) % 4
                if e:
                    arrived(i, y)
                for d in (1, 3, 2):
                    j = (y + d) % 4
                    go(copy(i, y, x, j, 18 + 3 * e + d), not_root(x, j))

        def finish():
            for d in (1, 3, 2):
                for e in range(4):
                    arrived((x + e) % 4, (y + d) % 4)

        return scatter, along_x, along_y, finish

    w_scatter, w_along_x, w_along_y, w_finish = make_spread(
        lambda i, j: wbuf.at[p, (i * 4 + j) // 2, j % 2], wsend, wrecv)
    l_scatter, l_along_x, l_along_y, l_finish = make_spread(
        lambda i, j: li.at[pl.ds(pl.multiple_of(p * 256 + (i * 4 + j) * 16, 16), 16)], lsend, lrecv)

    product(0)
    combine(0)

    @pl.when(is_root)
    def _():
        for g in range(8):
            for hl in range(2):
                wbuf[p, g, hl] = s_out[g, hl * 128:(hl + 1) * 128, :]

    w_scatter()
    product(1)
    combine(1)

    ms_ref = lambda c: ms.at[c]

    @pl.when(jnp.logical_and(others, z < 4))
    def _():
        ms[z % 4] = s_out[0, :, 0:128]

    src = jnp.logical_and(others, z < 4)
    for dr, to in ((0, zup), (1, zdn)):
        ref = ms.at[z % 4]
        go(remote(ref, ref, msend.at[0, dr], mrecv.at[z % 4], to), src)
    w_along_x()
    w_along_y()
    for d in range(1, 6):
        for dr, to in ((0, zup), (1, zdn)):
            i = (z + 8 - d) % 8 if dr == 0 else (z + d) % 8
            reach = up_of(i) if dr == 0 else 7 - up_of(i)
            ref = ms.at[i % 4]
            sem = mrecv.at[i % 4]
            pl.when(jnp.logical_and(others, jnp.logical_and(i < 4, d <= reach)))(
                functools.partial(wait_on, ref, sem))
            if d < 5:
                go(remote(ref, ref, msend.at[d, dr], sem, to),
                   jnp.logical_and(others, jnp.logical_and(i < 4, d < reach)))

    ii = lax.broadcasted_iota(jnp.int32, (128, 128), 0)
    jj = lax.broadcasted_iota(jnp.int32, (128, 128), 1)

    @pl.when(is_root)
    def _():
        gcopy.wait()
        li[...] = gsend[0:512, :] + grecv[0:512, :]
        for h in range(4):
            c = slice(h * 128, (h + 1) * 128)
            li[c, c] += jnp.where(ii == jj, lbuf[0, 0, h, KL:KL + 1, :], 0.0)
        for c in range(4):
            lanes = slice(c * 128, (c + 1) * 128)
            ms[c, 0:256, :] = li[pl.ds(pl.multiple_of(p * 256, 256), 256), lanes]
            ms[c, 256:512, :] += grecv[512:768, lanes]
        factor_lead(li, tile)
        for i in range(3):
            li[i * 128:(i + 1) * 128, (i + 1) * 128:512] = jnp.zeros((128, 384 - 128 * i), F32)

    l_scatter()
    l_along_x()
    w_finish()
    wcopy = remote(wbuf.at[p], wbuf.at[p], wsib.at[0], wsib.at[1], sib)
    wcopy.start()
    l_along_y()
    l_finish()
    mine_half = li.at[pl.ds(pl.multiple_of(p * 256, 256), 256)]
    lcopy = remote(mine_half, mine_half, lsib.at[0], lsib.at[1], sib)
    pl.when(others)(lcopy.start)
    wait_on(wbuf.at[1 - p], wsib.at[1])
    pl.when(others)(lambda: wait_on(li.at[pl.ds(pl.multiple_of((1 - p) * 256, 256), 256)], lsib.at[1]))

    hi, lo = split(li[...])
    lih[...] = hi
    lil[...] = lo
    row_ids = (x // 2) * 4 + y
    for k in range(4):
        n = (k + 1) * 128
        krows = slice(k * 128, n)
        acc = jnp.zeros((512, 128), F32)
        for c in range(k + 1):
            hi, lo = split(ms[c])
            cc = slice(c * 128, (c + 1) * 128)
            acc += nt(hi, lih[krows, cc]) + nt(lo, lih[krows, cc]) + nt(hi, lil[krows, cc])
        ri = lax.broadcasted_iota(jnp.int32, (512, 128), 0)
        ki = lax.broadcasted_iota(jnp.int32, (512, 128), 1) + k * 128
        rows_at = (((ri // 256) * 8 + row_ids) * 8 + (x_lo * 2 + p) * 2 + (ri // 128) % 2) * 128 + ri % 128
        acc = jnp.where(rows_at >= ki, acc, 0.0)
        hi, lo = split(acc)
        mfh[:, krows] = hi
        mfl[:, krows] = lo
        mf[k] = acc

    keep = jnp.logical_and(is_root, x_lo == 0)

    @pl.loop(0, 8)
    def _(g):
        hs, ls = [], []
        for q in range(2):
            for hl in range(2):
                hi, lo = split(wbuf[q, g, hl])
                hs.append(hi)
                ls.append(lo)
        wh = jnp.concatenate(hs, axis=0)
        wl = jnp.concatenate(ls, axis=0)
        f = mm(lih[...], wh) + mm(lil[...], wh) + mm(lih[...], wl)
        fh, fl = split(f)
        for a in range(2):
            rows = slice(a * 256, (a + 1) * 256)
            v = mm(mfh[rows, :], fh) + mm(mfl[rows, :], fh) + mm(mfh[rows, :], fl)
            sv = s_out[g, rows, :]
            v = jnp.where(jnp.logical_and(keep, a == 0), sv, sv - v)
            for c in range(2):
                out[pl.ds(a * 256 * 16 + c * 8 + g, 256, stride=16), :] = v[:, c * 128:(c + 1) * 128]

    for c in range(4):
        @pl.when(z == c)
        def _():
            out[pl.ds(0, 512, stride=16), :] = mf[c]

    for copy, cond in sends:
        if cond is None:
            copy.wait_send()
        else:
            pl.when(cond)(copy.wait_send)

    @pl.loop(0, 8)
    def _(g):
        for a in range(2):
            sib_copy(a, g).wait_send()

    wcopy.wait_send()
    pl.when(others)(lcopy.wait_send)


def schur_call(b):
    dma = pltpu.SemaphoreType.DMA
    vmem = pltpu.VMEM
    return pl.pallas_call(
        schur_kernel,
        out_shape=jax.ShapeDtypeStruct((8192, 128), F32),
        in_specs=[pl.BlockSpec(memory_space=pltpu.VMEM)],
        out_specs=pl.BlockSpec(memory_space=pltpu.VMEM),
        scratch_shapes=[
            vmem((2, 4, 4, KL, 128), F32), vmem((2, 2, 4, KP, 128), F32),
            vmem((1024, 2 * KL), BF16), vmem((1024, 2 * KL), BF16),
            vmem((2 * KL, 256), BF16), vmem((2 * KL, 256), BF16),
            vmem((8, 512, 256), F32), vmem((8, 512, 256), F32), vmem((8, 512, 256), F32),
            vmem((768, 512), F32), vmem((768, 512), F32), vmem((128, 128), F32),
            vmem((2, 8, 2, 128, 256), F32), vmem((512, 512), F32), vmem((4, 512, 128), F32), vmem((4, 512, 128), F32),
            vmem((512, 512), BF16), vmem((512, 512), BF16), vmem((512, 512), BF16), vmem((512, 512), BF16),
            dma((2, 3)), dma((2, 2)), dma((2, 4, 2)), dma((2, 4, 2)), dma((2, 2, 2, 2)),
            dma((4, 2, 2, 2, 2)), dma((2, 8)),
            dma((2, 4, 4)), dma((2, 4, 4, 2)), dma((2, 2, 4, 2)), dma((2, 8)),
            dma((2,)), dma((31,)), dma((4, 4)), dma((31,)), dma((4, 4)), dma((2,)), dma((2,)),
            dma((5, 2)), dma((4,)),
        ],
        compiler_params=pltpu.CompilerParams(
            collective_id=0, has_side_effects=True, vmem_limit_bytes=60 * 2**20
        ),
        name="schur_factor",
    )(b)


def scaled_blocks(link_block, block_mask, barrier_diag, first_section_diag):
    scen = block_mask.shape[0]
    w = block_mask.astype(F32).reshape(scen, 1, 2, 1) * jnp.sqrt(barrier_diag).reshape(scen, -1, 1, 1)
    v = (link_block.reshape(scen, -1, 2, 128) * w).reshape(KL, 2, 128).transpose(1, 0, 2)
    d = first_section_diag.reshape(2, 1, 128)
    return jnp.concatenate([v, d, jnp.zeros((2, KP - KL - 1, 128), F32)], axis=1)


def per_device(link_block, block_mask, barrier_diag, first_section_diag):
    b = scaled_blocks(link_block, block_mask, barrier_diag, first_section_diag)
    return schur_call(b).reshape(2, 1, 2, 128, 2, 8, 1, 128)


def solution(mesh):
    placed = (
        P("scen", None, "row", "col", None),
        P("scen", None, "row", "col"),
        P("scen"),
        P(None, "row", "col", None),
    )
    return jax.shard_map(
        per_device,
        mesh=mesh,
        in_specs=placed,
        out_specs=P(None, "row", "scen", None, None, None, "col", None),
        check_vma=False,
    )
```

```python
import functools
import jax
import jax.numpy as jnp
from jax import lax
from jax.experimental import pallas as pl
from jax.experimental.pallas import tpu as pltpu
from jax.sharding import PartitionSpec as P

PANEL = 256
F32 = jnp.float32
BF16 = jnp.bfloat16
KL = 640
KP = 648
NC = 3
CH = KP // NC
RING = 4


def place():
    s = lax.axis_index("scen")
    r = lax.axis_index("row")
    z = lax.axis_index("col")
    return (r // 4) * 2 + s // 2, r % 4, z, s % 2


def device(x, y, z, p):
    return ((x % 2) * 2 + p, (x // 2) * 4 + y, z)


def remote(src, dst, send, recv, to):
    return pltpu.make_async_remote_copy(
        src_ref=src, dst_ref=dst, send_sem=send, recv_sem=recv,
        device_id=to, device_id_type=pl.DeviceIdType.MESH,
    )


def split(v):
    hi = v.astype(BF16)
    return hi, (v - hi.astype(F32)).astype(BF16)


def mm(a, b):
    return jnp.dot(a, b, preferred_element_type=F32)


def nt(a, b):
    return lax.dot_general(a, b, (((1,), (1,)), ((), ())), preferred_element_type=F32)


def dot32(a, b):
    return jnp.dot(a, b, precision=lax.Precision.HIGHEST, preferred_element_type=F32)


def factor_tile(t):
    lanes = lax.broadcasted_iota(jnp.int32, (8, 128), 1)
    for p in range(0, 128, 8):
        n = 128 - p
        cols = [jnp.broadcast_to(t[p:128, p + j:p + j + 1], (n, 128)) for j in range(8)]
        row = t[p:p + 8, :]
        subl = lax.broadcasted_iota(jnp.int32, (8, 128), 0)
        us, rs_ = [], []
        for j in range(8):
            inv = lax.rsqrt(cols[j][j:j + 1, :])
            u = cols[j] * inv
            r = jnp.where(lanes[0:1] == p + j, inv, row[j:j + 1, :] * inv)
            scal = [u[m:m + 1, :] for m in range(8)]
            for m in range(j + 1, 8):
                cols[m] = cols[m] - u * scal[m]
            uj = jnp.where(subl > j, u[0:8, :], 0.0)
            base = jnp.where(jnp.logical_and(lanes == p + j, subl > j), 0.0, row)
            row = jnp.where(subl == j, jnp.broadcast_to(r, (8, 128)), base - uj * r)
            us.append(u)
        t[p:p + 8, :] = row
        if n > 8:
            rest = t[p + 8:128, :]
            rl_ = lax.broadcasted_iota(jnp.int32, (n - 8, 128), 1)
            rest = jnp.where(jnp.logical_and(rl_ >= p, rl_ < p + 8), 0.0, rest)
            for j in range(8):
                r = jnp.where(jnp.logical_and(lanes[0:1] > p + j, lanes[0:1] < p + 8), 0.0, row[j:j + 1, :])
                rest = rest - us[j][8:, :] * r
            t[p + 8:128, :] = rest


def factor_step(m, t, k):
    ii = lax.broadcasted_iota(jnp.int32, (128, 128), 0)
    jj = lax.broadcasted_iota(jnp.int32, (128, 128), 1)
    a, e = k * 128, (k + 1) * 128
    t[...] = m[a:e, a:e]
    factor_tile(t)
    inv = jnp.where(ii >= jj, t[...], 0.0)
    m[a:e, a:e] = inv
    for j in range(4):
        if j != k:
            m[a:e, j * 128:(j + 1) * 128] = dot32(inv, m[a:e, j * 128:(j + 1) * 128])
    for i in range(k + 1, 4):
        ut = m[a:e, i * 128:(i + 1) * 128].T
        r = slice(i * 128, (i + 1) * 128)
        for j in range(4):
            c = slice(j * 128, (j + 1) * 128)
            v = dot32(ut, m[a:e, c])
            m[r, c] = -v if j == k else m[r, c] - v


def schur_kernel(
    b, out, rbuf, lbuf, lthi, ltlo, rh, rl, pbuf, qbuf, s_out,
    gsend, grecv, tile, wbuf, li, ms, mf, lih, lil, mfh, mfl, fch, fcl,
    rs1, rs2, rs3, rr, rr2, ws1, ws2, ws3, wr, wr2, wsc, wrc,
    sp, lpeer, zs, lsem, sx, xsem, gsem, lsend, lrecv, wsib, lsib, msend, mrecv,
):
    x, y, z, p = place()
    plane = lambda i, j: device(i % 4, j % 4, z, p)
    zup = device(x, y, (z + 1) % 8, p)
    zdn = device(x, y, (z + 7) % 8, p)
    peer = device(x + 1 - 2 * (x % 2), y, z, p)
    sib = device(x, y, z, 1 - p)
    x_lo = x % 2
    rel = (z + 8 - 4 * x_lo) % 8
    is_src = rel < 4
    is_root = jnp.logical_and(x == 0, y == 0)
    others = jnp.logical_not(is_root)
    own_p = pl.multiple_of(p * 256, 256)
    sib_p = pl.multiple_of((1 - p) * 256, 256)

    barrier = pltpu.get_barrier_semaphore()
    partners = [plane(x + i, y + j) for i in range(4) for j in range(4) if i or j]
    partners += [zup, zdn, sib]
    for to in partners:
        pl.semaphore_signal(barrier, inc=1, device_id=to, device_id_type=pl.DeviceIdType.MESH)
    pl.semaphore_wait(barrier, len(partners))

    sends = []

    def go(copy, cond=None):
        if cond is None:
            copy.start()
        else:
            pl.when(cond)(copy.start)
        sends.append((copy, cond))

    def wait_on(ref, sem, cond=None):
        wait = pltpu.make_async_copy(ref, ref, sem).wait
        if cond is None:
            wait()
        else:
            pl.when(cond)(wait)

    def not_root(i, j):
        return jnp.logical_not(jnp.logical_and(i % 4 == 0, j % 4 == 0))

    class Gather:
        def __init__(self, blk, sub, s1, s2, s3, r, r2, rooted):
            self.blk, self.sub, self.s1, self.s2, self.s3, self.r, self.r2 = blk, sub, s1, s2, s3, r, r2
            self.rooted = rooted

        def at(self, a, d, e):
            return ((x + d) % 4, (y + e) % 4) if a == 0 else ((x + e) % 4, (y + d) % 4)

        def send(self, ref, send, recv, i, j):
            go(remote(ref, ref, send, recv, plane(i, j)), not_root(i, j) if self.rooted else None)

        def wait(self, ref, sem):
            wait_on(ref, sem, others if self.rooted else None)

        def first(self):
            for d in (1, 3, 2):
                for a in range(2):
                    self.send(self.blk(a, x, y), self.s1.at[a, d - 1], self.r.at[a, x, y], *self.at(a, d, 0))

        def second(self, a, k, d):
            i, j = self.at(a, d, 0)
            ref, sem = self.blk(a, i, j), self.r.at[a, i, j]
            if d:
                self.wait(ref, sem)
            self.send(ref, self.s2.at[a, k, 0], sem, *self.at(a, 0, 1))
            self.send(ref, self.s2.at[a, k, 1], sem, *self.at(a, 0, 3))

        def forward(self, a, k, d):
            for dr, e in ((0, 3), (1, 1)):
                i, j = self.at(a, d, e)
                self.wait(self.blk(a, i, j), self.r.at[a, i, j])
                line = i if a == 0 else j
                self.send(self.sub(a, i, j, dr), self.s3.at[a, k, dr], self.r2.at[a, line, dr],
                          *self.at(a, 0, 1 if dr == 0 else 3))

        def last(self, a, d):
            i, j = self.at(a, d, 2)
            line = i if a == 0 else j
            for dr in range(2):
                self.wait(self.sub(a, i, j, dr), self.r2.at[a, line, dr])

    right = Gather(
        lambda a, i, j: rbuf.at[a, i, j], lambda a, i, j, dr: rbuf.at[a, i, j, pl.ds(dr * 320, 320)],
        rs1, rs2, rs3, rr, rr2, False)
    lead = Gather(
        lambda a, i, j: wbuf.at[p, (i * 4 + j) // 2, j % 2, pl.ds(a * 64, 64)],
        lambda a, i, j, dr: wbuf.at[p, (i * 4 + j) // 2, j % 2, pl.ds(a * 64 + dr * 32, 32)],
        ws1, ws2, ws3, wr, wr2, True)

    for a in range(2):
        rbuf[a, x, y] = b[a, 0:KL, :]
        go(remote(b.at[a], lbuf.at[a, x_lo, z % 4], sp.at[a], lpeer.at[a], peer), jnp.logical_not(is_src))

    @pl.when(is_src)
    def _():
        for a in range(2):
            lbuf[a, x_lo, z % 4] = b[a]

    right.first()

    LAST = 4 * NC
    up_of = lambda i: jnp.where(i < 2, 2, 5)
    up1 = lambda v: jnp.where(jnp.logical_or(v == 0, v >= 4), 3, v - 1)
    up2 = lambda v: jnp.where(v >= 4, 2, v - 2)
    mirror = (11 - rel) % 8
    streams = []
    for dr in range(2):
        for k in range(2):
            v = rel if dr == 0 else mirror
            i = (up1 if k == 0 else up2)(v)
            valid = v >= 0 if k == 0 else v >= 2
            i = jnp.maximum(i, 0)
            d = (v + 8 - i) % 8
            src = i if dr == 0 else 3 - i
            streams.append((src, d, valid, jnp.logical_and(valid, d < up_of(i)), zup if dr == 0 else zdn))

    def zref(slot, c):
        a, k, h = c // (2 * NC), (c // NC) % 2, c % NC
        xl = (x_lo + k) % 2
        return lbuf.at[a, xl, slot, pl.ds(pl.multiple_of(h * CH, 8), CH)], lsem.at[a, xl, slot, h]

    def zsend(ref, sem, n, c, to):
        ring = zs.at[n, c % RING]

        @pl.when(c >= RING)
        def _():
            pltpu.make_async_copy(ref, ref, ring).wait()

        remote(ref, ref, ring, sem, to).start()

    def zown(c):
        @pl.when(is_src)
        def _():
            ref, sem = zref(z % 4, c)

            @pl.when(c % (2 * NC) == NC)
            def _():
                whole = lbuf.at[c // (2 * NC), 1 - x_lo, z % 4]
                pltpu.make_async_copy(whole, whole, lpeer.at[c // (2 * NC)]).wait()

            zsend(ref, sem, 4, c, zup)
            zsend(ref, sem, 5, c, zdn)

    def zstep(t):
        @pl.when(t + 2 < LAST)
        def _():
            zown(t + 2)

        for n, (src, d, valid, passes, to) in enumerate(streams):
            c = t - d + 1

            @pl.when(jnp.logical_and(valid, jnp.logical_and(c >= 0, c < LAST)))
            def _():
                ref, sem = zref(src, c)
                wait_on(ref, sem)

                @pl.when(passes)
                def _():
                    zsend(ref, sem, n, c, to)

    def zsteps(lo, hi):
        @pl.loop(lo, hi)
        def _(t):
            zstep(t)

    def zdrain():
        ref, _ = zref(0, 0)
        for n in range(6):
            cond = is_src if n >= 4 else streams[n][3]

            @pl.when(cond)
            def _():
                for q in range(RING):
                    pltpu.make_async_copy(ref, ref, zs.at[n, q]).wait()

    def turn(a):
        @pl.loop(0, 4)
        def _(hh):
            rb = pl.multiple_of(((hh // 2) * 4 + a * 2 + hh % 2) * 128, 128)
            for xl in range(2):
                hi, lo = split(lbuf[a, xl, hh, 0:KL, :].T)
                lthi[pl.ds(rb, 128), xl * KL:(xl + 1) * KL] = hi
                ltlo[pl.ds(rb, 128), xl * KL:(xl + 1) * KL] = lo

    gcopy = remote(gsend, grecv, gsem.at[0], gsem.at[1], sib)

    def gram(rows, j):
        cols = slice(j * 512, j * 512 + 256)
        return nt(lthi[rows, :], lthi[cols, :]) + nt(lthi[rows, :], ltlo[cols, :]) + nt(ltlo[rows, :], lthi[cols, :])

    def lead_products():
        for j in range(2):
            for i in range(2):
                gsend[i * 256:i * 256 + 256, j * 256:j * 256 + 256] = gram(slice(i * 512, i * 512 + 256), j)
        gcopy.start()

    ii = lax.broadcasted_iota(jnp.int32, (128, 128), 0)
    jj = lax.broadcasted_iota(jnp.int32, (128, 128), 1)

    def lead_matrix():
        gcopy.wait()
        li[...] = gsend[...] + grecv[...]
        for h in range(4):
            c = slice(h * 128, (h + 1) * 128)
            li[c, c] += jnp.where(ii == jj, lbuf[0, 0, h, KL:KL + 1, :], 0.0)

    def sib_copy(a, g):
        rows = pl.ds(a * 256, 256)
        return remote(pbuf.at[g, rows], qbuf.at[g, rows], sx.at[a, g], xsem.at[a, g], sib)

    def product(a, g):
        for xl in range(2):
            for c in range(2):
                hi, lo = split(rbuf[c, (g // 4) * 2 + xl, g % 4])
                rh[xl * KL:(xl + 1) * KL, c * 128:(c + 1) * 128] = hi
                rl[xl * KL:(xl + 1) * KL, c * 128:(c + 1) * 128] = lo
        for t in range(2):
            q = (1 - p) if t == 0 else p
            rows = pl.ds(pl.multiple_of(q * 512 + a * 256, 256), 256)
            v = mm(lthi[rows, :], rh[...]) + mm(ltlo[rows, :], rh[...]) + mm(lthi[rows, :], rl[...])
            if t == 0:
                pbuf[g, a * 256:(a + 1) * 256, :] = v
                sib_copy(a, g).start()
            else:
                s_out[g, a * 256:(a + 1) * 256, :] = v

    def products(a, lo, hi):
        @pl.loop(lo, hi)
        def _(k):
            product(a, k)

    g_own = (x // 2) * 4 + y

    def combine(a, g):
        rows = slice(a * 256, a * 256 + 256)
        sib_copy(a, g).wait_recv()
        s_out[g, rows, :] = s_out[g, rows, :] + qbuf[g, rows, :]

    def add_diag(a):
        @pl.when(z // 2 == x_lo * 2 + p)
        def _():
            here = pl.ds(pl.multiple_of(a * 256 + (z % 2) * 128, 128), 128)
            diag = jnp.where(ii == jj, b[a, KL:KL + 1, :], 0.0)
            s_out[g_own, here, a * 128:(a + 1) * 128] += diag

    def piece(i, j):
        return li.at[pl.ds(pl.multiple_of(p * 256 + (i * 4 + j) * 16, 16), 16)]

    def l_copy(i, j, to_i, to_j, slot):
        ref = piece(i, j)
        return remote(ref, ref, lsend.at[slot], lrecv.at[i, j], plane(to_i, to_j))

    def l_scatter():
        for k in range(1, 16):
            go(l_copy(k // 4, k % 4, k // 4, k % 4, k), is_root)

    def l_arrived(i, j):
        wait_on(piece(i, j), lrecv.at[i, j], others)

    def l_along_x():
        l_arrived(x, y)
        for d in (1, 3, 2):
            go(l_copy(x, y, (x + d) % 4, y, 15 + d), not_root(x + d, y))

    def l_along_y():
        for e in range(4):
            i = (x + e) % 4
            if e:
                l_arrived(i, y)
            for d in (1, 3, 2):
                go(l_copy(i, y, x, (y + d) % 4, 18 + 3 * e + d), not_root(x, y + d))

    def l_finish():
        for d in (1, 3, 2):
            for e in range(4):
                l_arrived((x + e) % 4, (y + d) % 4)

    def on_root(f, *args):
        pl.when(is_root)(functools.partial(f, *args))

    def m_ref(i, a):
        return ms.at[i, pl.ds(a * 256, 256)]

    def m_first(a):
        @pl.when(z < 4)
        def _():
            ms[z % 4, a * 256:(a + 1) * 256, :] = s_out[0, a * 256:(a + 1) * 256, 0:128]

        for dr, to in ((0, zup), (1, zdn)):
            ref = m_ref(z % 4, a)
            go(remote(ref, ref, msend.at[a, 0, dr], mrecv.at[a, z % 4], to), z < 4)

    def m_forward(a, d):
        for dr, to in ((0, zup), (1, zdn)):
            i = (z + 8 - d) % 8 if dr == 0 else (z + d) % 8
            reach = up_of(i) if dr == 0 else 7 - up_of(i)
            ref, sem = m_ref(i % 4, a), mrecv.at[a, i % 4]
            wait_on(ref, sem, jnp.logical_and(i < 4, d <= reach))
            if d < 5:
                go(remote(ref, ref, msend.at[a, d, dr], sem, to), jnp.logical_and(i < 4, d < reach))

    def lead_zero():
        for i in range(3):
            li[i * 128:(i + 1) * 128, (i + 1) * 128:512] = jnp.zeros((128, 384 - 128 * i), F32)

    def combines(a, lo, hi):
        @pl.loop(lo, hi)
        def _(g):
            combine(a, g)

    def w_scatter():
        @pl.when(is_root)
        def _():
            for g in range(8):
                for hl in range(2):
                    wbuf[p, g, hl] = s_out[g, hl * 128:(hl + 1) * 128, :]

        for k in range(1, 16):
            ref = wbuf.at[p, k // 2, k % 2]
            go(remote(ref, ref, wsc.at[k], wrc.at[0], plane(k // 4, k % 4)), is_root)

    def both(f, *args):
        for a in range(2):
            f(a, *args)

    wcopy = remote(wbuf.at[p], wbuf.at[p], wsib.at[0], wsib.at[1], sib)
    mine_half = li.at[pl.ds(own_p, 256)]
    lcopy = remote(mine_half, mine_half, lsib.at[0], lsib.at[1], sib)

    zown(0)
    zown(1)
    both(right.second, 0, 0)
    zsteps(0, 3)
    both(right.second, 1, 1)
    both(right.second, 2, 3)
    zsteps(3, 4)
    both(right.second, 3, 2)
    both(right.forward, 0, 0)
    zsteps(4, 5)
    both(right.forward, 1, 1)
    zsteps(5, 7)
    both(right.forward, 2, 3)
    zsteps(7, 9)
    both(right.forward, 3, 2)
    zsteps(9, 10)
    turn(0)
    on_root(lead_products)
    zsteps(10, 11)
    for d in (0, 1, 3, 2):
        both(right.last, d)
    products(0, 0, 4)
    zsteps(11, 12)
    products(0, 4, 8)
    combines(0, 0, 8)
    add_diag(0)
    w_scatter()
    zsteps(12, 13)
    m_first(0)
    on_root(lead_matrix)
    on_root(factor_step, li, tile, 0)
    zsteps(13, 14)
    m_forward(0, 1)
    wait_on(wbuf.at[p, (x * 4 + y) // 2, y % 2], wrc.at[0], others)
    lead.first()
    both(lead.second, 0, 0)
    on_root(factor_step, li, tile, 1)
    zsteps(14, 15)
    m_forward(0, 2)
    both(lead.second, 1, 1)
    both(lead.second, 2, 3)
    on_root(factor_step, li, tile, 2)
    zsteps(15, 16)
    m_forward(0, 3)
    both(lead.second, 3, 2)
    both(lead.forward, 0, 0)
    turn(1)
    products(1, 0, 1)
    combines(1, 0, 1)
    pl.when(g_own == 0)(functools.partial(add_diag, 1))
    m_first(1)
    on_root(factor_step, li, tile, 3)
    on_root(lead_zero)
    l_scatter()
    m_forward(0, 4)
    both(lead.forward, 1, 1)
    products(1, 1, 3)
    m_forward(1, 1)
    both(lead.forward, 2, 3)
    both(lead.forward, 3, 2)
    products(1, 3, 5)
    m_forward(1, 2)
    m_forward(0, 5)
    l_along_x()
    products(1, 5, 7)
    m_forward(1, 3)
    for d in (0, 1, 3, 2):
        both(lead.last, d)
    wcopy.start()
    l_along_y()
    products(1, 7, 8)
    m_forward(1, 4)
    combines(1, 1, 8)
    pl.when(g_own != 0)(functools.partial(add_diag, 1))
    l_finish()
    pl.when(others)(lcopy.start)
    wait_on(wbuf.at[1 - p], wsib.at[1])
    wait_on(li.at[pl.ds(sib_p, 256)], lsib.at[1], others)

    hi, lo = split(li[...])
    lih[...] = hi
    lil[...] = lo

    @pl.loop(0, 8)
    def _(g):
        hs, ls = [], []
        for q in range(2):
            for hl in range(2):
                hi, lo = split(wbuf[q, g, hl])
                hs.append(hi)
                ls.append(lo)
        wh = jnp.concatenate(hs, axis=0)
        wl = jnp.concatenate(ls, axis=0)
        hi, lo = split(mm(lih[...], wh) + mm(lil[...], wh) + mm(lih[...], wl))
        fch[g] = hi
        fcl[g] = lo

    m_forward(1, 5)
    for k in range(4):
        krows = slice(k * 128, (k + 1) * 128)
        acc = jnp.zeros((512, 128), F32)
        for c in range(k + 1):
            hi, lo = split(ms[c])
            cc = slice(c * 128, (c + 1) * 128)
            acc += nt(hi, lih[krows, cc]) + nt(lo, lih[krows, cc]) + nt(hi, lil[krows, cc])
        ri = lax.broadcasted_iota(jnp.int32, (512, 128), 0)
        ki = lax.broadcasted_iota(jnp.int32, (512, 128), 1) + k * 128
        rows_at = (((ri // 256) * 8 + g_own) * 8 + (x_lo * 2 + p) * 2 + (ri // 128) % 2) * 128 + ri % 128
        acc = jnp.where(rows_at >= ki, acc, 0.0)
        hi, lo = split(acc)
        mfh[:, krows] = hi
        mfl[:, krows] = lo
        mf[k] = acc

    @pl.loop(0, 8)
    def _(g):
        for a in range(2):
            rows = slice(a * 256, (a + 1) * 256)
            v = mm(mfh[rows, :], fch[g]) + mm(mfl[rows, :], fch[g]) + mm(mfh[rows, :], fcl[g])
            sv = s_out[g, rows, :]
            v = jnp.where(jnp.logical_and(is_root, a == 0), sv, sv - v)
            for c in range(2):
                out[pl.ds(a * 256 * 16 + c * 8 + g, 256, stride=16), :] = v[:, c * 128:(c + 1) * 128]

    for c in range(4):
        @pl.when(z == c)
        def _():
            out[pl.ds(0, 512, stride=16), :] = mf[c]

    zdrain()
    for copy, cond in sends:
        if cond is None:
            copy.wait_send()
        else:
            pl.when(cond)(copy.wait_send)

    @pl.loop(0, 8)
    def _(g):
        for a in range(2):
            sib_copy(a, g).wait_send()

    wcopy.wait_send()
    pl.when(others)(lcopy.wait_send)


def schur_call(b):
    dma = pltpu.SemaphoreType.DMA
    vmem = pltpu.VMEM
    return pl.pallas_call(
        schur_kernel,
        out_shape=jax.ShapeDtypeStruct((8192, 128), F32),
        in_specs=[pl.BlockSpec(memory_space=pltpu.VMEM)],
        out_specs=pl.BlockSpec(memory_space=pltpu.VMEM),
        scratch_shapes=[
            vmem((2, 4, 4, KL, 128), F32), vmem((2, 2, 4, KP, 128), F32),
            vmem((1024, 2 * KL), BF16), vmem((1024, 2 * KL), BF16),
            vmem((2 * KL, 256), BF16), vmem((2 * KL, 256), BF16),
            vmem((8, 512, 256), F32), vmem((8, 512, 256), F32), vmem((8, 512, 256), F32),
            vmem((512, 512), F32), vmem((512, 512), F32), vmem((128, 128), F32),
            vmem((2, 8, 2, 128, 256), F32), vmem((512, 512), F32), vmem((4, 512, 128), F32), vmem((4, 512, 128), F32),
            vmem((512, 512), BF16), vmem((512, 512), BF16), vmem((512, 512), BF16), vmem((512, 512), BF16),
            vmem((8, 512, 256), BF16), vmem((8, 512, 256), BF16),
            dma((2, 3)), dma((2, 4, 2)), dma((2, 4, 2)), dma((2, 4, 4)), dma((2, 4, 2)),
            dma((2, 3)), dma((2, 4, 2)), dma((2, 4, 2)), dma((2, 4, 4)), dma((2, 4, 2)),
            dma((16,)), dma((1,)),
            dma((2,)), dma((2,)), dma((6, RING)), dma((2, 2, 4, NC)),
            dma((2, 8)), dma((2, 8)), dma((2,)), dma((31,)), dma((4, 4)), dma((2,)), dma((2,)),
            dma((2, 5, 2)), dma((2, 4)),
        ],
        compiler_params=pltpu.CompilerParams(
            collective_id=0, has_side_effects=True, vmem_limit_bytes=60 * 2**20
        ),
        name="schur_factor",
    )(b)


def scaled_blocks(link_block, block_mask, barrier_diag, first_section_diag):
    scen = block_mask.shape[0]
    w = block_mask.astype(F32).reshape(scen, 1, 2, 1) * jnp.sqrt(barrier_diag).reshape(scen, -1, 1, 1)
    v = (link_block.reshape(scen, -1, 2, 128) * w).reshape(KL, 2, 128).transpose(1, 0, 2)
    d = first_section_diag.reshape(2, 1, 128)
    return jnp.concatenate([v, d, jnp.zeros((2, KP - KL - 1, 128), F32)], axis=1)


def per_device(link_block, block_mask, barrier_diag, first_section_diag):
    b = scaled_blocks(link_block, block_mask, barrier_diag, first_section_diag)
    return schur_call(b).reshape(2, 1, 2, 128, 2, 8, 1, 128)


def solution(mesh):
    placed = (
        P("scen", None, "row", "col", None),
        P("scen", None, "row", "col"),
        P("scen"),
        P(None, "row", "col", None),
    )
    return jax.shard_map(
        per_device,
        mesh=mesh,
        in_specs=placed,
        out_specs=P(None, "row", "scen", None, None, None, "col", None),
        check_vma=False,
    )
```

```python
import functools
import jax
import jax.numpy as jnp
from jax import lax
from jax.experimental import pallas as pl
from jax.experimental.pallas import tpu as pltpu
from jax.sharding import PartitionSpec as P

PANEL = 256
F32 = jnp.float32
BF16 = jnp.bfloat16
KL = 640
KP = 648
NC = 3
CH = KP // NC
RING = 4


def place():
    s = lax.axis_index("scen")
    r = lax.axis_index("row")
    z = lax.axis_index("col")
    return (r // 4) * 2 + s // 2, r % 4, z, s % 2


def device(x, y, z, p):
    return ((x % 2) * 2 + p, (x // 2) * 4 + y, z)


def remote(src, dst, send, recv, to):
    return pltpu.make_async_remote_copy(
        src_ref=src, dst_ref=dst, send_sem=send, recv_sem=recv,
        device_id=to, device_id_type=pl.DeviceIdType.MESH,
    )


def split(v):
    hi = v.astype(BF16)
    return hi, (v - hi.astype(F32)).astype(BF16)


def mm(a, b):
    return jnp.dot(a, b, preferred_element_type=F32)


def nt(a, b):
    return lax.dot_general(a, b, (((1,), (1,)), ((), ())), preferred_element_type=F32)


def dot32(a, b):
    return jnp.dot(a, b, precision=lax.Precision.HIGHEST, preferred_element_type=F32)


def factor_tile(t):
    lanes = lax.broadcasted_iota(jnp.int32, (8, 128), 1)
    for p in range(0, 128, 8):
        n = 128 - p
        cols = [jnp.broadcast_to(t[p:128, p + j:p + j + 1], (n, 128)) for j in range(8)]
        row = t[p:p + 8, :]
        subl = lax.broadcasted_iota(jnp.int32, (8, 128), 0)
        us, rs_ = [], []
        for j in range(8):
            inv = lax.rsqrt(cols[j][j:j + 1, :])
            u = cols[j] * inv
            r = jnp.where(lanes[0:1] == p + j, inv, row[j:j + 1, :] * inv)
            scal = [u[m:m + 1, :] for m in range(8)]
            for m in range(j + 1, 8):
                cols[m] = cols[m] - u * scal[m]
            uj = jnp.where(subl > j, u[0:8, :], 0.0)
            base = jnp.where(jnp.logical_and(lanes == p + j, subl > j), 0.0, row)
            row = jnp.where(subl == j, jnp.broadcast_to(r, (8, 128)), base - uj * r)
            us.append(u)
        t[p:p + 8, :] = row
        if n > 8:
            rest = t[p + 8:128, :]
            rl_ = lax.broadcasted_iota(jnp.int32, (n - 8, 128), 1)
            rest = jnp.where(jnp.logical_and(rl_ >= p, rl_ < p + 8), 0.0, rest)
            for j in range(8):
                r = jnp.where(jnp.logical_and(lanes[0:1] > p + j, lanes[0:1] < p + 8), 0.0, row[j:j + 1, :])
                rest = rest - us[j][8:, :] * r
            t[p + 8:128, :] = rest


def factor_step(m, t, k):
    ii = lax.broadcasted_iota(jnp.int32, (128, 128), 0)
    jj = lax.broadcasted_iota(jnp.int32, (128, 128), 1)
    a, e = k * 128, (k + 1) * 128
    t[...] = m[a:e, a:e]
    factor_tile(t)
    inv = jnp.where(ii >= jj, t[...], 0.0)
    m[a:e, a:e] = inv
    for j in range(4):
        if j != k:
            m[a:e, j * 128:(j + 1) * 128] = dot32(inv, m[a:e, j * 128:(j + 1) * 128])
    for i in range(k + 1, 4):
        ut = m[a:e, i * 128:(i + 1) * 128].T
        r = slice(i * 128, (i + 1) * 128)
        for j in range(4):
            c = slice(j * 128, (j + 1) * 128)
            v = dot32(ut, m[a:e, c])
            m[r, c] = -v if j == k else m[r, c] - v


def schur_kernel(
    b, out, rbuf, lbuf, lthi, ltlo, rh, rl, pbuf, qbuf, s_out,
    gsend, grecv, tile, wbuf, li, ms, mf, lih, lil, mfh, mfl, fch, fcl,
    rs1, rs2, rs3, rr, rr2, ws1, ws2, ws3, wr, wr2, wsc, wrc,
    sp, lpeer, zs, lsem, sx, xsem, gsem, lsend, lrecv, wsib, lsib, msend, mrecv,
):
    x, y, z, p = place()
    plane = lambda i, j: device(i % 4, j % 4, z, p)
    zup = device(x, y, (z + 1) % 8, p)
    zdn = device(x, y, (z + 7) % 8, p)
    peer = device(x + 1 - 2 * (x % 2), y, z, p)
    sib = device(x, y, z, 1 - p)
    x_lo = x % 2
    rel = (z + 8 - 4 * x_lo) % 8
    is_src = rel < 4
    is_root = jnp.logical_and(x == 0, y == 0)
    others = jnp.logical_not(is_root)
    own_p = pl.multiple_of(p * 256, 256)
    sib_p = pl.multiple_of((1 - p) * 256, 256)

    barrier = pltpu.get_barrier_semaphore()
    partners = [plane(x + i, y + j) for i in range(4) for j in range(4) if i or j]
    partners += [zup, zdn, sib]
    for to in partners:
        pl.semaphore_signal(barrier, inc=1, device_id=to, device_id_type=pl.DeviceIdType.MESH)
    pl.semaphore_wait(barrier, len(partners))

    sends = []

    def go(copy, cond=None):
        if cond is None:
            copy.start()
        else:
            pl.when(cond)(copy.start)
        sends.append((copy, cond))

    def wait_on(ref, sem, cond=None):
        wait = pltpu.make_async_copy(ref, ref, sem).wait
        if cond is None:
            wait()
        else:
            pl.when(cond)(wait)

    def not_root(i, j):
        return jnp.logical_not(jnp.logical_and(i % 4 == 0, j % 4 == 0))

    class Gather:
        def __init__(self, blk, sub, s1, s2, s3, r, r2, rooted):
            self.blk, self.sub, self.s1, self.s2, self.s3, self.r, self.r2 = blk, sub, s1, s2, s3, r, r2
            self.rooted = rooted

        def at(self, a, d, e):
            return ((x + d) % 4, (y + e) % 4) if a == 0 else ((x + e) % 4, (y + d) % 4)

        def send(self, ref, send, recv, i, j):
            go(remote(ref, ref, send, recv, plane(i, j)), not_root(i, j) if self.rooted else None)

        def wait(self, ref, sem):
            wait_on(ref, sem, others if self.rooted else None)

        def first(self):
            for d in (1, 3, 2):
                for a in range(2):
                    self.send(self.blk(a, x, y), self.s1.at[a, d - 1], self.r.at[a, x, y], *self.at(a, d, 0))

        def second(self, a, k, d):
            i, j = self.at(a, d, 0)
            ref, sem = self.blk(a, i, j), self.r.at[a, i, j]
            if d:
                self.wait(ref, sem)
            self.send(ref, self.s2.at[a, k, 0], sem, *self.at(a, 0, 1))
            self.send(ref, self.s2.at[a, k, 1], sem, *self.at(a, 0, 3))

        def forward(self, a, k, d):
            for dr, e in ((0, 3), (1, 1)):
                i, j = self.at(a, d, e)
                self.wait(self.blk(a, i, j), self.r.at[a, i, j])
                line = i if a == 0 else j
                self.send(self.sub(a, i, j, dr), self.s3.at[a, k, dr], self.r2.at[a, line, dr],
                          *self.at(a, 0, 1 if dr == 0 else 3))

        def last(self, a, d):
            i, j = self.at(a, d, 2)
            line = i if a == 0 else j
            for dr in range(2):
                self.wait(self.sub(a, i, j, dr), self.r2.at[a, line, dr])

    right = Gather(
        lambda a, i, j: rbuf.at[a, i, j], lambda a, i, j, dr: rbuf.at[a, i, j, pl.ds(dr * 320, 320)],
        rs1, rs2, rs3, rr, rr2, False)
    lead = Gather(
        lambda a, i, j: wbuf.at[p, (i * 4 + j) // 2, j % 2, pl.ds(a * 64, 64)],
        lambda a, i, j, dr: wbuf.at[p, (i * 4 + j) // 2, j % 2, pl.ds(a * 64 + dr * 32, 32)],
        ws1, ws2, ws3, wr, wr2, True)

    for a in range(2):
        rbuf[a, x, y] = b[a, 0:KL, :]
        go(remote(b.at[a], lbuf.at[a, x_lo, z % 4], sp.at[a], lpeer.at[a], peer), jnp.logical_not(is_src))

    @pl.when(is_src)
    def _():
        for a in range(2):
            lbuf[a, x_lo, z % 4] = b[a]

    right.first()

    LAST = 4 * NC
    up_of = lambda i: jnp.where(i < 2, 2, 5)
    up1 = lambda v: jnp.where(jnp.logical_or(v == 0, v >= 4), 3, v - 1)
    up2 = lambda v: jnp.where(v >= 4, 2, v - 2)
    mirror = (11 - rel) % 8
    streams = []
    for dr in range(2):
        for k in range(2):
            v = rel if dr == 0 else mirror
            i = (up1 if k == 0 else up2)(v)
            valid = v >= 0 if k == 0 else v >= 2
            i = jnp.maximum(i, 0)
            d = (v + 8 - i) % 8
            src = i if dr == 0 else 3 - i
            streams.append((src, d, valid, jnp.logical_and(valid, d < up_of(i)), zup if dr == 0 else zdn))

    def zref(slot, c):
        a, k, h = c // (2 * NC), (c // NC) % 2, c % NC
        xl = (x_lo + k) % 2
        return lbuf.at[a, xl, slot, pl.ds(pl.multiple_of(h * CH, 8), CH)], lsem.at[a, xl, slot, h]

    def zsend(ref, sem, n, c, to):
        ring = zs.at[n, c % RING]

        @pl.when(c >= RING)
        def _():
            pltpu.make_async_copy(ref, ref, ring).wait()

        remote(ref, ref, ring, sem, to).start()

    def zown(c):
        @pl.when(is_src)
        def _():
            ref, sem = zref(z % 4, c)

            @pl.when(c % (2 * NC) == NC)
            def _():
                whole = lbuf.at[c // (2 * NC), 1 - x_lo, z % 4]
                pltpu.make_async_copy(whole, whole, lpeer.at[c // (2 * NC)]).wait()

            zsend(ref, sem, 4, c, zup)
            zsend(ref, sem, 5, c, zdn)

    def zstep(t):
        @pl.when(t + 2 < LAST)
        def _():
            zown(t + 2)

        for n, (src, d, valid, passes, to) in enumerate(streams):
            c = t - d + 1

            @pl.when(jnp.logical_and(valid, jnp.logical_and(c >= 0, c < LAST)))
            def _():
                ref, sem = zref(src, c)
                wait_on(ref, sem)

                @pl.when(passes)
                def _():
                    zsend(ref, sem, n, c, to)

    def zsteps(lo, hi):
        @pl.loop(lo, hi)
        def _(t):
            zstep(t)

    def zdrain():
        ref, _ = zref(0, 0)
        for n in range(6):
            cond = is_src if n >= 4 else streams[n][3]

            @pl.when(cond)
            def _():
                for q in range(RING):
                    pltpu.make_async_copy(ref, ref, zs.at[n, q]).wait()

    def turn(a):
        @pl.loop(0, 4)
        def _(hh):
            rb = pl.multiple_of(((hh // 2) * 4 + a * 2 + hh % 2) * 128, 128)
            for xl in range(2):
                hi, lo = split(lbuf[a, xl, hh, 0:KL, :].T)
                lthi[pl.ds(rb, 128), xl * KL:(xl + 1) * KL] = hi
                ltlo[pl.ds(rb, 128), xl * KL:(xl + 1) * KL] = lo

    gcopy = remote(gsend, grecv, gsem.at[0], gsem.at[1], sib)

    def gram(rows, j):
        cols = slice(j * 512, j * 512 + 256)
        return nt(lthi[rows, :], lthi[cols, :]) + nt(lthi[rows, :], ltlo[cols, :]) + nt(ltlo[rows, :], lthi[cols, :])

    def lead_products():
        for j in range(2):
            for i in range(2):
                gsend[i * 256:i * 256 + 256, j * 256:j * 256 + 256] = gram(slice(i * 512, i * 512 + 256), j)
        gcopy.start()

    ii = lax.broadcasted_iota(jnp.int32, (128, 128), 0)
    jj = lax.broadcasted_iota(jnp.int32, (128, 128), 1)

    def lead_matrix():
        gcopy.wait()
        li[...] = gsend[...] + grecv[...]
        for h in range(4):
            c = slice(h * 128, (h + 1) * 128)
            li[c, c] += jnp.where(ii == jj, lbuf[0, 0, h, KL:KL + 1, :], 0.0)

    def sib_copy(a, g):
        rows = pl.ds(a * 256, 256)
        return remote(pbuf.at[g, rows], qbuf.at[g, rows], sx.at[a, g], xsem.at[a, g], sib)

    def product(a, g):
        for xl in range(2):
            for c in range(2):
                hi, lo = split(rbuf[c, (g // 4) * 2 + xl, g % 4])
                rh[xl * KL:(xl + 1) * KL, c * 128:(c + 1) * 128] = hi
                rl[xl * KL:(xl + 1) * KL, c * 128:(c + 1) * 128] = lo
        tiles = []
        for t in range(2):
            q = (1 - p) if t == 0 else p
            rows = pl.ds(pl.multiple_of(q * 512 + a * 256, 256), 256)
            tiles.append(mm(lthi[rows, :], rh[...]) + mm(ltlo[rows, :], rh[...]) + mm(lthi[rows, :], rl[...]))
        s_out[g, a * 256:(a + 1) * 256, :] = tiles[1]
        pbuf[g, a * 256:(a + 1) * 256, :] = tiles[0]
        sib_copy(a, g).start()

    def products(a, lo, hi):
        @pl.loop(lo, hi)
        def _(k):
            product(a, k)

    g_own = (x // 2) * 4 + y

    def combine(a, g):
        rows = slice(a * 256, a * 256 + 256)
        sib_copy(a, g).wait_recv()
        s_out[g, rows, :] = s_out[g, rows, :] + qbuf[g, rows, :]

    def add_diag(a):
        @pl.when(z // 2 == x_lo * 2 + p)
        def _():
            here = pl.ds(pl.multiple_of(a * 256 + (z % 2) * 128, 128), 128)
            diag = jnp.where(ii == jj, b[a, KL:KL + 1, :], 0.0)
            s_out[g_own, here, a * 128:(a + 1) * 128] += diag

    def piece(i, j):
        return li.at[pl.ds(pl.multiple_of(p * 256 + (i * 4 + j) * 16, 16), 16)]

    def l_copy(i, j, to_i, to_j, slot):
        ref = piece(i, j)
        return remote(ref, ref, lsend.at[slot], lrecv.at[i, j], plane(to_i, to_j))

    def l_scatter():
        for k in range(1, 16):
            go(l_copy(k // 4, k % 4, k // 4, k % 4, k), is_root)

    def l_arrived(i, j):
        wait_on(piece(i, j), lrecv.at[i, j], others)

    def l_along_x():
        l_arrived(x, y)
        for d in (1, 3, 2):
            go(l_copy(x, y, (x + d) % 4, y, 15 + d), not_root(x + d, y))

    def l_along_y():
        for e in range(4):
            i = (x + e) % 4
            if e:
                l_arrived(i, y)
            for d in (1, 3, 2):
                go(l_copy(i, y, x, (y + d) % 4, 18 + 3 * e + d), not_root(x, y + d))

    def l_finish():
        for d in (1, 3, 2):
            for e in range(4):
                l_arrived((x + e) % 4, (y + d) % 4)

    def on_root(f, *args):
        pl.when(is_root)(functools.partial(f, *args))

    def m_ref(i, a):
        return ms.at[i, pl.ds(a * 256, 256)]

    def m_first(a):
        @pl.when(z < 4)
        def _():
            ms[z % 4, a * 256:(a + 1) * 256, :] = s_out[0, a * 256:(a + 1) * 256, 0:128]

        for dr, to in ((0, zup), (1, zdn)):
            ref = m_ref(z % 4, a)
            go(remote(ref, ref, msend.at[a, 0, dr], mrecv.at[a, z % 4], to), z < 4)

    def m_forward(a, d):
        for dr, to in ((0, zup), (1, zdn)):
            i = (z + 8 - d) % 8 if dr == 0 else (z + d) % 8
            reach = up_of(i) if dr == 0 else 7 - up_of(i)
            ref, sem = m_ref(i % 4, a), mrecv.at[a, i % 4]
            wait_on(ref, sem, jnp.logical_and(i < 4, d <= reach))
            if d < 5:
                go(remote(ref, ref, msend.at[a, d, dr], sem, to), jnp.logical_and(i < 4, d < reach))

    def lead_zero():
        for i in range(3):
            li[i * 128:(i + 1) * 128, (i + 1) * 128:512] = jnp.zeros((128, 384 - 128 * i), F32)

    def combines(a, lo, hi):
        @pl.loop(lo, hi)
        def _(g):
            combine(a, g)

    def w_scatter():
        @pl.when(is_root)
        def _():
            for g in range(8):
                for hl in range(2):
                    wbuf[p, g, hl] = s_out[g, hl * 128:(hl + 1) * 128, :]

        for k in range(1, 16):
            ref = wbuf.at[p, k // 2, k % 2]
            go(remote(ref, ref, wsc.at[k], wrc.at[0], plane(k // 4, k % 4)), is_root)

    def both(f, *args):
        for a in range(2):
            f(a, *args)

    wcopy = remote(wbuf.at[p], wbuf.at[p], wsib.at[0], wsib.at[1], sib)
    mine_half = li.at[pl.ds(own_p, 256)]
    lcopy = remote(mine_half, mine_half, lsib.at[0], lsib.at[1], sib)

    zown(0)
    zown(1)
    both(right.second, 0, 0)
    zsteps(0, 3)
    both(right.second, 1, 1)
    both(right.second, 2, 3)
    zsteps(3, 4)
    both(right.second, 3, 2)
    both(right.forward, 0, 0)
    zsteps(4, 5)
    both(right.forward, 1, 1)
    zsteps(5, 7)
    both(right.forward, 2, 3)
    zsteps(7, 9)
    both(right.forward, 3, 2)
    zsteps(9, 10)
    turn(0)
    on_root(lead_products)
    zsteps(10, 11)
    for d in (0, 1, 3, 2):
        both(right.last, d)
    products(0, 0, 4)
    zsteps(11, 12)
    products(0, 4, 8)
    combines(0, 0, 8)
    add_diag(0)
    w_scatter()
    zsteps(12, 13)
    m_first(0)
    on_root(lead_matrix)
    on_root(factor_step, li, tile, 0)
    zsteps(13, 14)
    m_forward(0, 1)
    on_root(factor_step, li, tile, 1)
    zsteps(14, 15)
    m_forward(0, 2)
    on_root(factor_step, li, tile, 2)
    zsteps(15, 16)
    m_forward(0, 3)
    on_root(factor_step, li, tile, 3)
    on_root(lead_zero)
    l_scatter()
    wait_on(wbuf.at[p, (x * 4 + y) // 2, y % 2], wrc.at[0], others)
    lead.first()
    both(lead.second, 0, 0)
    turn(1)
    products(1, 0, 1)
    combines(1, 0, 1)
    pl.when(g_own == 0)(functools.partial(add_diag, 1))
    m_first(1)
    m_forward(0, 4)
    both(lead.second, 1, 1)
    both(lead.second, 2, 3)
    both(lead.second, 3, 2)
    l_along_x()
    both(lead.forward, 0, 0)
    products(1, 1, 3)
    m_forward(1, 1)
    both(lead.forward, 1, 1)
    both(lead.forward, 2, 3)
    l_along_y()
    both(lead.forward, 3, 2)
    m_forward(1, 2)
    products(1, 3, 5)
    m_forward(0, 5)
    m_forward(1, 3)
    l_finish()
    pl.when(others)(lcopy.start)
    for d in (0, 1, 3, 2):
        both(lead.last, d)
    wcopy.start()
    m_forward(1, 4)
    products(1, 5, 8)
    combines(1, 1, 8)
    pl.when(g_own != 0)(functools.partial(add_diag, 1))
    wait_on(li.at[pl.ds(sib_p, 256)], lsib.at[1], others)
    wait_on(wbuf.at[1 - p], wsib.at[1])

    hi, lo = split(li[...])
    lih[...] = hi
    lil[...] = lo

    @pl.loop(0, 8)
    def _(g):
        hs, ls = [], []
        for q in range(2):
            for hl in range(2):
                hi, lo = split(wbuf[q, g, hl])
                hs.append(hi)
                ls.append(lo)
        wh = jnp.concatenate(hs, axis=0)
        wl = jnp.concatenate(ls, axis=0)
        hi, lo = split(mm(lih[...], wh) + mm(lil[...], wh) + mm(lih[...], wl))
        fch[g] = hi
        fcl[g] = lo

    m_forward(1, 5)
    for k in range(4):
        krows = slice(k * 128, (k + 1) * 128)
        acc = jnp.zeros((512, 128), F32)
        for c in range(k + 1):
            hi, lo = split(ms[c])
            cc = slice(c * 128, (c + 1) * 128)
            acc += nt(hi, lih[krows, cc]) + nt(lo, lih[krows, cc]) + nt(hi, lil[krows, cc])
        ri = lax.broadcasted_iota(jnp.int32, (512, 128), 0)
        ki = lax.broadcasted_iota(jnp.int32, (512, 128), 1) + k * 128
        rows_at = (((ri // 256) * 8 + g_own) * 8 + (x_lo * 2 + p) * 2 + (ri // 128) % 2) * 128 + ri % 128
        acc = jnp.where(rows_at >= ki, acc, 0.0)
        hi, lo = split(acc)
        mfh[:, krows] = hi
        mfl[:, krows] = lo
        mf[k] = acc

    @pl.loop(0, 8)
    def _(g):
        for a in range(2):
            rows = slice(a * 256, (a + 1) * 256)
            v = mm(mfh[rows, :], fch[g]) + mm(mfl[rows, :], fch[g]) + mm(mfh[rows, :], fcl[g])
            sv = s_out[g, rows, :]
            v = jnp.where(jnp.logical_and(is_root, a == 0), sv, sv - v)
            for c in range(2):
                out[pl.ds(a * 256 * 16 + c * 8 + g, 256, stride=16), :] = v[:, c * 128:(c + 1) * 128]

    for c in range(4):
        @pl.when(z == c)
        def _():
            out[pl.ds(0, 512, stride=16), :] = mf[c]

    zdrain()
    for copy, cond in sends:
        if cond is None:
            copy.wait_send()
        else:
            pl.when(cond)(copy.wait_send)

    @pl.loop(0, 8)
    def _(g):
        for a in range(2):
            sib_copy(a, g).wait_send()

    wcopy.wait_send()
    pl.when(others)(lcopy.wait_send)


def schur_call(b):
    dma = pltpu.SemaphoreType.DMA
    vmem = pltpu.VMEM
    return pl.pallas_call(
        schur_kernel,
        out_shape=jax.ShapeDtypeStruct((8192, 128), F32),
        in_specs=[pl.BlockSpec(memory_space=pltpu.VMEM)],
        out_specs=pl.BlockSpec(memory_space=pltpu.VMEM),
        scratch_shapes=[
            vmem((2, 4, 4, KL, 128), F32), vmem((2, 2, 4, KP, 128), F32),
            vmem((1024, 2 * KL), BF16), vmem((1024, 2 * KL), BF16),
            vmem((2 * KL, 256), BF16), vmem((2 * KL, 256), BF16),
            vmem((8, 512, 256), F32), vmem((8, 512, 256), F32), vmem((8, 512, 256), F32),
            vmem((512, 512), F32), vmem((512, 512), F32), vmem((128, 128), F32),
            vmem((2, 8, 2, 128, 256), F32), vmem((512, 512), F32), vmem((4, 512, 128), F32), vmem((4, 512, 128), F32),
            vmem((512, 512), BF16), vmem((512, 512), BF16), vmem((512, 512), BF16), vmem((512, 512), BF16),
            vmem((8, 512, 256), BF16), vmem((8, 512, 256), BF16),
            dma((2, 3)), dma((2, 4, 2)), dma((2, 4, 2)), dma((2, 4, 4)), dma((2, 4, 2)),
            dma((2, 3)), dma((2, 4, 2)), dma((2, 4, 2)), dma((2, 4, 4)), dma((2, 4, 2)),
            dma((16,)), dma((1,)),
            dma((2,)), dma((2,)), dma((6, RING)), dma((2, 2, 4, NC)),
            dma((2, 8)), dma((2, 8)), dma((2,)), dma((31,)), dma((4, 4)), dma((2,)), dma((2,)),
            dma((2, 5, 2)), dma((2, 4)),
        ],
        compiler_params=pltpu.CompilerParams(
            collective_id=0, has_side_effects=True, vmem_limit_bytes=60 * 2**20
        ),
        name="schur_factor",
    )(b)


def scaled_blocks(link_block, block_mask, barrier_diag, first_section_diag):
    scen = block_mask.shape[0]
    w = block_mask.astype(F32).reshape(scen, 1, 2, 1) * jnp.sqrt(barrier_diag).reshape(scen, -1, 1, 1)
    v = (link_block.reshape(scen, -1, 2, 128) * w).reshape(KL, 2, 128).transpose(1, 0, 2)
    d = first_section_diag.reshape(2, 1, 128)
    return jnp.concatenate([v, d, jnp.zeros((2, KP - KL - 1, 128), F32)], axis=1)


def per_device(link_block, block_mask, barrier_diag, first_section_diag):
    b = scaled_blocks(link_block, block_mask, barrier_diag, first_section_diag)
    return schur_call(b).reshape(2, 1, 2, 128, 2, 8, 1, 128)


def solution(mesh):
    placed = (
        P("scen", None, "row", "col", None),
        P("scen", None, "row", "col"),
        P("scen"),
        P(None, "row", "col", None),
    )
    return jax.shard_map(
        per_device,
        mesh=mesh,
        in_specs=placed,
        out_specs=P(None, "row", "scen", None, None, None, "col", None),
        check_vma=False,
    )
```

```python
import functools
import jax
import jax.numpy as jnp
from jax import lax
from jax.experimental import pallas as pl
from jax.experimental.pallas import tpu as pltpu
from jax.sharding import PartitionSpec as P

PANEL = 256
F32 = jnp.float32
BF16 = jnp.bfloat16
KL = 640
KP = 648
NC = 3
CH = KP // NC
RING = 4


def place():
    s = lax.axis_index("scen")
    r = lax.axis_index("row")
    z = lax.axis_index("col")
    return (r // 4) * 2 + s // 2, r % 4, z, s % 2


def device(x, y, z, p):
    return ((x % 2) * 2 + p, (x // 2) * 4 + y, z)


def remote(src, dst, send, recv, to):
    return pltpu.make_async_remote_copy(
        src_ref=src, dst_ref=dst, send_sem=send, recv_sem=recv,
        device_id=to, device_id_type=pl.DeviceIdType.MESH,
    )


def split(v):
    hi = v.astype(BF16)
    return hi, (v - hi.astype(F32)).astype(BF16)


def mm(a, b):
    return jnp.dot(a, b, preferred_element_type=F32)


def nt(a, b):
    return lax.dot_general(a, b, (((1,), (1,)), ((), ())), preferred_element_type=F32)


def dot32(a, b):
    return jnp.dot(a, b, precision=lax.Precision.HIGHEST, preferred_element_type=F32)


def factor_tile(t):
    lanes = lax.broadcasted_iota(jnp.int32, (8, 128), 1)
    for p in range(0, 128, 8):
        n = 128 - p
        cols = [jnp.broadcast_to(t[p:128, p + j:p + j + 1], (n, 128)) for j in range(8)]
        row = t[p:p + 8, :]
        subl = lax.broadcasted_iota(jnp.int32, (8, 128), 0)
        us, rs_ = [], []
        for j in range(8):
            inv = lax.rsqrt(cols[j][j:j + 1, :])
            u = cols[j] * inv
            r = jnp.where(lanes[0:1] == p + j, inv, row[j:j + 1, :] * inv)
            scal = [u[m:m + 1, :] for m in range(8)]
            for m in range(j + 1, 8):
                cols[m] = cols[m] - u * scal[m]
            uj = jnp.where(subl > j, u[0:8, :], 0.0)
            base = jnp.where(jnp.logical_and(lanes == p + j, subl > j), 0.0, row)
            row = jnp.where(subl == j, jnp.broadcast_to(r, (8, 128)), base - uj * r)
            us.append(u)
        t[p:p + 8, :] = row
        if n > 8:
            rest = t[p + 8:128, :]
            rl_ = lax.broadcasted_iota(jnp.int32, (n - 8, 128), 1)
            rest = jnp.where(jnp.logical_and(rl_ >= p, rl_ < p + 8), 0.0, rest)
            for j in range(8):
                r = jnp.where(jnp.logical_and(lanes[0:1] > p + j, lanes[0:1] < p + 8), 0.0, row[j:j + 1, :])
                rest = rest - us[j][8:, :] * r
            t[p + 8:128, :] = rest


def factor_step(m, t, k):
    ii = lax.broadcasted_iota(jnp.int32, (128, 128), 0)
    jj = lax.broadcasted_iota(jnp.int32, (128, 128), 1)
    a, e = k * 128, (k + 1) * 128
    t[...] = m[a:e, a:e]
    factor_tile(t)
    inv = jnp.where(ii >= jj, t[...], 0.0)
    m[a:e, a:e] = inv
    for j in range(4):
        if j != k:
            m[a:e, j * 128:(j + 1) * 128] = dot32(inv, m[a:e, j * 128:(j + 1) * 128])
    for i in range(k + 1, 4):
        ut = m[a:e, i * 128:(i + 1) * 128].T
        r = slice(i * 128, (i + 1) * 128)
        for j in range(4):
            c = slice(j * 128, (j + 1) * 128)
            v = dot32(ut, m[a:e, c])
            m[r, c] = -v if j == k else m[r, c] - v


def schur_kernel(
    b, out, rbuf, lbuf, lthi, ltlo, rh, rl, pbuf, qbuf, s_out,
    gsend, grecv, tile, wbuf, li, ms, mf, lih, lil, mfh, mfl, fch, fcl,
    rs1, rs2, rs3, rr, rr2, ws1, ws2, ws3, wr, wr2, wsc, wrc,
    sp, lpeer, zs, lsem, sx, xsem, gsem, lsend, lrecv, wsib, lsib, msend, mrecv,
):
    x, y, z, p = place()
    plane = lambda i, j: device(i % 4, j % 4, z, p)
    zup = device(x, y, (z + 1) % 8, p)
    zdn = device(x, y, (z + 7) % 8, p)
    peer = device(x + 1 - 2 * (x % 2), y, z, p)
    sib = device(x, y, z, 1 - p)
    x_lo = x % 2
    rel = (z + 8 - 4 * x_lo) % 8
    is_src = rel < 4
    is_root = jnp.logical_and(x == 0, y == 0)
    others = jnp.logical_not(is_root)
    own_p = pl.multiple_of(p * 256, 256)
    sib_p = pl.multiple_of((1 - p) * 256, 256)

    barrier = pltpu.get_barrier_semaphore()
    partners = [plane(x + i, y + j) for i in range(4) for j in range(4) if i or j]
    partners += [zup, zdn, sib]
    for to in partners:
        pl.semaphore_signal(barrier, inc=1, device_id=to, device_id_type=pl.DeviceIdType.MESH)
    pl.semaphore_wait(barrier, len(partners))

    sends = []

    def go(copy, cond=None):
        if cond is None:
            copy.start()
        else:
            pl.when(cond)(copy.start)
        sends.append((copy, cond))

    def wait_on(ref, sem, cond=None):
        wait = pltpu.make_async_copy(ref, ref, sem).wait
        if cond is None:
            wait()
        else:
            pl.when(cond)(wait)

    def not_root(i, j):
        return jnp.logical_not(jnp.logical_and(i % 4 == 0, j % 4 == 0))

    class Gather:
        def __init__(self, blk, sub, s1, s2, s3, r, r2, rooted):
            self.blk, self.sub, self.s1, self.s2, self.s3, self.r, self.r2 = blk, sub, s1, s2, s3, r, r2
            self.rooted = rooted

        def at(self, a, d, e):
            return ((x + d) % 4, (y + e) % 4) if a == 0 else ((x + e) % 4, (y + d) % 4)

        def send(self, ref, send, recv, i, j):
            go(remote(ref, ref, send, recv, plane(i, j)), not_root(i, j) if self.rooted else None)

        def wait(self, ref, sem):
            wait_on(ref, sem, others if self.rooted else None)

        def first(self):
            for d in (1, 3, 2):
                for a in range(2):
                    self.send(self.blk(a, x, y), self.s1.at[a, d - 1], self.r.at[a, x, y], *self.at(a, d, 0))

        def second(self, a, k, d):
            i, j = self.at(a, d, 0)
            ref, sem = self.blk(a, i, j), self.r.at[a, i, j]
            if d:
                self.wait(ref, sem)
            self.send(ref, self.s2.at[a, k, 0], sem, *self.at(a, 0, 1))
            self.send(ref, self.s2.at[a, k, 1], sem, *self.at(a, 0, 3))

        def forward(self, a, k, d):
            for dr, e in ((0, 3), (1, 1)):
                i, j = self.at(a, d, e)
                self.wait(self.blk(a, i, j), self.r.at[a, i, j])
                line = i if a == 0 else j
                self.send(self.sub(a, i, j, dr), self.s3.at[a, k, dr], self.r2.at[a, line, dr],
                          *self.at(a, 0, 1 if dr == 0 else 3))

        def last(self, a, d):
            i, j = self.at(a, d, 2)
            line = i if a == 0 else j
            for dr in range(2):
                self.wait(self.sub(a, i, j, dr), self.r2.at[a, line, dr])

    right = Gather(
        lambda a, i, j: rbuf.at[a, i, j], lambda a, i, j, dr: rbuf.at[a, i, j, pl.ds(dr * 320, 320)],
        rs1, rs2, rs3, rr, rr2, False)
    lead = Gather(
        lambda a, i, j: wbuf.at[p, (i * 4 + j) // 2, j % 2, pl.ds(a * 64, 64)],
        lambda a, i, j, dr: wbuf.at[p, (i * 4 + j) // 2, j % 2, pl.ds(a * 64 + dr * 32, 32)],
        ws1, ws2, ws3, wr, wr2, True)

    for a in range(2):
        rbuf[a, x, y] = b[a, 0:KL, :]
        go(remote(b.at[a], lbuf.at[a, x_lo, z % 4], sp.at[a], lpeer.at[a], peer), jnp.logical_not(is_src))

    @pl.when(is_src)
    def _():
        for a in range(2):
            lbuf[a, x_lo, z % 4] = b[a]

    right.first()

    LAST = 4 * NC
    up_of = lambda i: jnp.where(i < 2, 2, 5)
    up1 = lambda v: jnp.where(jnp.logical_or(v == 0, v >= 4), 3, v - 1)
    up2 = lambda v: jnp.where(v >= 4, 2, v - 2)
    mirror = (11 - rel) % 8
    streams = []
    for dr in range(2):
        for k in range(2):
            v = rel if dr == 0 else mirror
            i = (up1 if k == 0 else up2)(v)
            valid = v >= 0 if k == 0 else v >= 2
            i = jnp.maximum(i, 0)
            d = (v + 8 - i) % 8
            src = i if dr == 0 else 3 - i
            streams.append((src, d, valid, jnp.logical_and(valid, d < up_of(i)), zup if dr == 0 else zdn))

    def zref(slot, c):
        a, k, h = c // (2 * NC), (c // NC) % 2, c % NC
        xl = (x_lo + k) % 2
        return lbuf.at[a, xl, slot, pl.ds(pl.multiple_of(h * CH, 8), CH)], lsem.at[a, xl, slot, h]

    def zsend(ref, sem, n, c, to):
        ring = zs.at[n, c % RING]

        @pl.when(c >= RING)
        def _():
            pltpu.make_async_copy(ref, ref, ring).wait()

        remote(ref, ref, ring, sem, to).start()

    def zown(c):
        @pl.when(is_src)
        def _():
            ref, sem = zref(z % 4, c)

            @pl.when(c % (2 * NC) == NC)
            def _():
                whole = lbuf.at[c // (2 * NC), 1 - x_lo, z % 4]
                pltpu.make_async_copy(whole, whole, lpeer.at[c // (2 * NC)]).wait()

            zsend(ref, sem, 4, c, zup)
            zsend(ref, sem, 5, c, zdn)

    def zstep(t):
        @pl.when(t + 2 < LAST)
        def _():
            zown(t + 2)

        for n, (src, d, valid, passes, to) in enumerate(streams):
            c = t - d + 1

            @pl.when(jnp.logical_and(valid, jnp.logical_and(c >= 0, c < LAST)))
            def _():
                ref, sem = zref(src, c)
                wait_on(ref, sem)

                @pl.when(passes)
                def _():
                    zsend(ref, sem, n, c, to)

    def zsteps(lo, hi):
        @pl.loop(lo, hi)
        def _(t):
            zstep(t)

    def zdrain():
        ref, _ = zref(0, 0)
        for n in range(6):
            cond = is_src if n >= 4 else streams[n][3]

            @pl.when(cond)
            def _():
                for q in range(RING):
                    pltpu.make_async_copy(ref, ref, zs.at[n, q]).wait()

    def turn(a):
        @pl.loop(0, 4)
        def _(hh):
            rb = pl.multiple_of(((hh // 2) * 4 + a * 2 + hh % 2) * 128, 128)
            for xl in range(2):
                hi, lo = split(lbuf[a, xl, hh, 0:KL, :].T)
                lthi[pl.ds(rb, 128), xl * KL:(xl + 1) * KL] = hi
                ltlo[pl.ds(rb, 128), xl * KL:(xl + 1) * KL] = lo

    gcopy = remote(gsend, grecv, gsem.at[0], gsem.at[1], sib)

    def gram(rows, j):
        cols = slice(j * 512, j * 512 + 256)
        return nt(lthi[rows, :], lthi[cols, :]) + nt(lthi[rows, :], ltlo[cols, :]) + nt(ltlo[rows, :], lthi[cols, :])

    def lead_products():
        for j in range(2):
            for i in range(2):
                gsend[i * 256:i * 256 + 256, j * 256:j * 256 + 256] = gram(slice(i * 512, i * 512 + 256), j)
        gcopy.start()

    ii = lax.broadcasted_iota(jnp.int32, (128, 128), 0)
    jj = lax.broadcasted_iota(jnp.int32, (128, 128), 1)

    def lead_matrix():
        gcopy.wait()
        li[...] = gsend[...] + grecv[...]
        for h in range(4):
            c = slice(h * 128, (h + 1) * 128)
            li[c, c] += jnp.where(ii == jj, lbuf[0, 0, h, KL:KL + 1, :], 0.0)

    def sib_copy(a, g):
        rows = pl.ds(a * 256, 256)
        return remote(pbuf.at[g, rows], qbuf.at[g, rows], sx.at[a, g], xsem.at[a, g], sib)

    def product(a, g):
        for xl in range(2):
            for c in range(2):
                hi, lo = split(rbuf[c, (g // 4) * 2 + xl, g % 4])
                rh[xl * KL:(xl + 1) * KL, c * 128:(c + 1) * 128] = hi
                rl[xl * KL:(xl + 1) * KL, c * 128:(c + 1) * 128] = lo
        tiles = []
        for t in range(2):
            q = (1 - p) if t == 0 else p
            rows = pl.ds(pl.multiple_of(q * 512 + a * 256, 256), 256)
            tiles.append(mm(lthi[rows, :], rh[...]) + mm(ltlo[rows, :], rh[...]) + mm(lthi[rows, :], rl[...]))
        s_out[g, a * 256:(a + 1) * 256, :] = tiles[1]
        pbuf[g, a * 256:(a + 1) * 256, :] = tiles[0]
        sib_copy(a, g).start()

    def products(a, lo, hi):
        @pl.loop(lo, hi)
        def _(k):
            product(a, k)

    g_own = (x // 2) * 4 + y

    def combine(a, g):
        rows = slice(a * 256, a * 256 + 256)
        sib_copy(a, g).wait_recv()
        s_out[g, rows, :] = s_out[g, rows, :] + qbuf[g, rows, :]

    def add_diag(a):
        @pl.when(z // 2 == x_lo * 2 + p)
        def _():
            here = pl.ds(pl.multiple_of(a * 256 + (z % 2) * 128, 128), 128)
            diag = jnp.where(ii == jj, b[a, KL:KL + 1, :], 0.0)
            s_out[g_own, here, a * 128:(a + 1) * 128] += diag

    def piece(i, j):
        return li.at[pl.ds(pl.multiple_of(p * 256 + (i * 4 + j) * 16, 16), 16)]

    def l_copy(i, j, to_i, to_j, slot):
        ref = piece(i, j)
        return remote(ref, ref, lsend.at[slot], lrecv.at[i, j], plane(to_i, to_j))

    def l_scatter():
        for k in range(1, 16):
            go(l_copy(k // 4, k % 4, k // 4, k % 4, k), is_root)

    def l_arrived(i, j):
        wait_on(piece(i, j), lrecv.at[i, j], others)

    def l_along_x():
        l_arrived(x, y)
        for d in (1, 3, 2):
            go(l_copy(x, y, (x + d) % 4, y, 15 + d), not_root(x + d, y))

    def l_along_y():
        for e in range(4):
            i = (x + e) % 4
            if e:
                l_arrived(i, y)
            for d in (1, 3, 2):
                go(l_copy(i, y, x, (y + d) % 4, 18 + 3 * e + d), not_root(x, y + d))

    def l_finish():
        for d in (1, 3, 2):
            for e in range(4):
                l_arrived((x + e) % 4, (y + d) % 4)

    def on_root(f, *args):
        pl.when(is_root)(functools.partial(f, *args))

    def m_ref(i, a):
        return ms.at[i, pl.ds(a * 256, 256)]

    def m_first(a):
        @pl.when(z < 4)
        def _():
            ms[z % 4, a * 256:(a + 1) * 256, :] = s_out[0, a * 256:(a + 1) * 256, 0:128]

        for dr, to in ((0, zup), (1, zdn)):
            ref = m_ref(z % 4, a)
            go(remote(ref, ref, msend.at[a, 0, dr], mrecv.at[a, z % 4], to), z < 4)

    def m_forward(a, d):
        for dr, to in ((0, zup), (1, zdn)):
            i = (z + 8 - d) % 8 if dr == 0 else (z + d) % 8
            reach = up_of(i) if dr == 0 else 7 - up_of(i)
            ref, sem = m_ref(i % 4, a), mrecv.at[a, i % 4]
            wait_on(ref, sem, jnp.logical_and(i < 4, d <= reach))
            if d < 5:
                go(remote(ref, ref, msend.at[a, d, dr], sem, to), jnp.logical_and(i < 4, d < reach))

    def lead_zero():
        for i in range(3):
            li[i * 128:(i + 1) * 128, (i + 1) * 128:512] = jnp.zeros((128, 384 - 128 * i), F32)

    def combines(a, lo, hi):
        @pl.loop(lo, hi)
        def _(g):
            combine(a, g)

    def w_scatter():
        @pl.when(is_root)
        def _():
            for g in range(8):
                for hl in range(2):
                    wbuf[p, g, hl] = s_out[g, hl * 128:(hl + 1) * 128, :]

        for k in range(1, 16):
            ref = wbuf.at[p, k // 2, k % 2]
            go(remote(ref, ref, wsc.at[k], wrc.at[0], plane(k // 4, k % 4)), is_root)

    def both(f, *args):
        for a in range(2):
            f(a, *args)

    wcopy = remote(wbuf.at[p], wbuf.at[p], wsib.at[0], wsib.at[1], sib)
    mine_half = li.at[pl.ds(own_p, 256)]
    lcopy = remote(mine_half, mine_half, lsib.at[0], lsib.at[1], sib)

    zown(0)
    zown(1)
    both(right.second, 0, 0)
    zsteps(0, 3)
    both(right.second, 1, 1)
    both(right.second, 2, 3)
    zsteps(3, 4)
    both(right.second, 3, 2)
    both(right.forward, 0, 0)
    zsteps(4, 5)
    both(right.forward, 1, 1)
    zsteps(5, 7)
    both(right.forward, 2, 3)
    zsteps(7, 9)
    both(right.forward, 3, 2)
    zsteps(9, 10)
    turn(0)
    on_root(lead_products)
    zsteps(10, 11)
    for d in (0, 1, 3, 2):
        both(right.last, d)
    products(0, 0, 4)
    zsteps(11, 12)
    products(0, 4, 8)
    combines(0, 0, 8)
    add_diag(0)
    w_scatter()
    zsteps(12, 13)
    m_first(0)
    on_root(lead_matrix)
    on_root(factor_step, li, tile, 0)
    zsteps(13, 14)
    m_forward(0, 1)
    on_root(factor_step, li, tile, 1)
    zsteps(14, 15)
    m_forward(0, 2)
    on_root(factor_step, li, tile, 2)
    zsteps(15, 16)
    m_forward(0, 3)
    on_root(factor_step, li, tile, 3)
    on_root(lead_zero)
    l_scatter()
    wait_on(wbuf.at[p, (x * 4 + y) // 2, y % 2], wrc.at[0], others)
    lead.first()
    both(lead.second, 0, 0)
    turn(1)
    products(1, 0, 1)
    combines(1, 0, 1)
    pl.when(g_own == 0)(functools.partial(add_diag, 1))
    m_first(1)
    m_forward(0, 4)
    both(lead.second, 1, 1)
    both(lead.second, 2, 3)
    both(lead.second, 3, 2)
    l_along_x()
    both(lead.forward, 0, 0)
    products(1, 1, 3)
    m_forward(1, 1)
    both(lead.forward, 1, 1)
    both(lead.forward, 2, 3)
    l_along_y()
    both(lead.forward, 3, 2)
    m_forward(1, 2)
    products(1, 3, 5)
    m_forward(0, 5)
    m_forward(1, 3)
    l_finish()
    pl.when(others)(lcopy.start)
    for d in (0, 1, 3, 2):
        both(lead.last, d)
    wcopy.start()
    m_forward(1, 4)
    products(1, 5, 8)
    combines(1, 1, 8)
    pl.when(g_own != 0)(functools.partial(add_diag, 1))
    wait_on(li.at[pl.ds(sib_p, 256)], lsib.at[1], others)
    wait_on(wbuf.at[1 - p], wsib.at[1])

    hi, lo = split(li[...])
    lih[...] = hi
    lil[...] = lo

    @pl.loop(0, 8)
    def _(g):
        hs, ls = [], []
        for q in range(2):
            for hl in range(2):
                hi, lo = split(wbuf[q, g, hl])
                hs.append(hi)
                ls.append(lo)
        wh = jnp.concatenate(hs, axis=0)
        wl = jnp.concatenate(ls, axis=0)
        hi, lo = split(mm(lih[...], wh) + mm(lil[...], wh) + mm(lih[...], wl))
        fch[g] = hi
        fcl[g] = lo

    m_forward(1, 5)
    for k in range(4):
        krows = slice(k * 128, (k + 1) * 128)
        acc = jnp.zeros((512, 128), F32)
        for c in range(k + 1):
            hi, lo = split(ms[c])
            cc = slice(c * 128, (c + 1) * 128)
            acc += nt(hi, lih[krows, cc]) + nt(lo, lih[krows, cc]) + nt(hi, lil[krows, cc])
        ri = lax.broadcasted_iota(jnp.int32, (512, 128), 0)
        ki = lax.broadcasted_iota(jnp.int32, (512, 128), 1) + k * 128
        rows_at = (((ri // 256) * 8 + g_own) * 8 + (x_lo * 2 + p) * 2 + (ri // 128) % 2) * 128 + ri % 128
        acc = jnp.where(rows_at >= ki, acc, 0.0)
        hi, lo = split(acc)
        mfh[:, krows] = hi
        mfl[:, krows] = lo
        mf[k] = acc

    @pl.loop(0, 8)
    def _(g):
        for a in range(2):
            rows = slice(a * 256, (a + 1) * 256)
            v = mm(mfh[rows, :], fch[g]) + mm(mfl[rows, :], fch[g]) + mm(mfh[rows, :], fcl[g])
            sv = s_out[g, rows, :]
            v = jnp.where(jnp.logical_and(is_root, a == 0), sv, sv - v)
            for c in range(2):
                out[pl.ds(a * 256 * 16 + c * 8 + g, 256, stride=16), :] = v[:, c * 128:(c + 1) * 128]

    for c in range(4):
        @pl.when(z == c)
        def _():
            out[pl.ds(0, 512, stride=16), :] = mf[c]

    zdrain()
    for copy, cond in sends:
        if cond is None:
            copy.wait_send()
        else:
            pl.when(cond)(copy.wait_send)

    @pl.loop(0, 8)
    def _(g):
        for a in range(2):
            sib_copy(a, g).wait_send()

    wcopy.wait_send()
    pl.when(others)(lcopy.wait_send)


def schur_call(b):
    dma = pltpu.SemaphoreType.DMA
    vmem = pltpu.VMEM
    return pl.pallas_call(
        schur_kernel,
        out_shape=jax.ShapeDtypeStruct((8192, 128), F32),
        in_specs=[pl.BlockSpec(memory_space=pltpu.VMEM)],
        out_specs=pl.BlockSpec(memory_space=pltpu.VMEM),
        scratch_shapes=[
            vmem((2, 4, 4, KL, 128), F32), vmem((2, 2, 4, KP, 128), F32),
            vmem((1024, 2 * KL), BF16), vmem((1024, 2 * KL), BF16),
            vmem((2 * KL, 256), BF16), vmem((2 * KL, 256), BF16),
            vmem((8, 512, 256), F32), vmem((8, 512, 256), F32), vmem((8, 512, 256), F32),
            vmem((512, 512), F32), vmem((512, 512), F32), vmem((128, 128), F32),
            vmem((2, 8, 2, 128, 256), F32), vmem((512, 512), F32), vmem((4, 512, 128), F32), vmem((4, 512, 128), F32),
            vmem((512, 512), BF16), vmem((512, 512), BF16), vmem((512, 512), BF16), vmem((512, 512), BF16),
            vmem((8, 512, 256), BF16), vmem((8, 512, 256), BF16),
            dma((2, 3)), dma((2, 4, 2)), dma((2, 4, 2)), dma((2, 4, 4)), dma((2, 4, 2)),
            dma((2, 3)), dma((2, 4, 2)), dma((2, 4, 2)), dma((2, 4, 4)), dma((2, 4, 2)),
            dma((16,)), dma((1,)),
            dma((2,)), dma((2,)), dma((6, RING)), dma((2, 2, 4, NC)),
            dma((2, 8)), dma((2, 8)), dma((2,)), dma((31,)), dma((4, 4)), dma((2,)), dma((2,)),
            dma((2, 5, 2)), dma((2, 4)),
        ],
        compiler_params=pltpu.CompilerParams(
            collective_id=0, has_side_effects=True, vmem_limit_bytes=60 * 2**20
        ),
        name="schur_factor",
    )(b)


def hand_over(src, dst):
    dst[...] = src[...]


def hand_over_call(v):
    spec = pl.BlockSpec((2048, 128), lambda i: (i, 0))
    return pl.pallas_call(
        hand_over,
        grid=(4,),
        out_shape=jax.ShapeDtypeStruct(v.shape, v.dtype),
        in_specs=[spec],
        out_specs=spec,
        name="hand_over",
    )(v)


def scaled_blocks(link_block, block_mask, barrier_diag, first_section_diag):
    scen = block_mask.shape[0]
    w = block_mask.astype(F32).reshape(scen, 1, 2, 1) * jnp.sqrt(barrier_diag).reshape(scen, -1, 1, 1)
    v = (link_block.reshape(scen, -1, 2, 128) * w).reshape(KL, 2, 128).transpose(1, 0, 2)
    d = first_section_diag.reshape(2, 1, 128)
    return jnp.concatenate([v, d, jnp.zeros((2, KP - KL - 1, 128), F32)], axis=1)


def per_device(link_block, block_mask, barrier_diag, first_section_diag):
    b = scaled_blocks(link_block, block_mask, barrier_diag, first_section_diag)
    return hand_over_call(schur_call(b)).reshape(2, 1, 2, 128, 2, 8, 1, 128)


def solution(mesh):
    placed = (
        P("scen", None, "row", "col", None),
        P("scen", None, "row", "col"),
        P("scen"),
        P(None, "row", "col", None),
    )
    return jax.shard_map(
        per_device,
        mesh=mesh,
        in_specs=placed,
        out_specs=P(None, "row", "scen", None, None, None, "col", None),
        check_vma=False,
    )
```
